128 devices in a mesh: row: 16 (over x_lo, z, core), col: 8 (over x_hi, y).
Axes of the slice: x: 4 (x_hi: 2, x_lo: 2; x = x_hi * 2 + x_lo), y: 4, z: 4, core: 2. Of those that a mesh axis runs over, the one named last changes fastest.
Arguments:
- atom_pos: float32 [2, 3, 16384], P(None, None, ('row', 'col')), may hold values from -5 to 5
- noise: float32 [2, 3, 16384], P(None, None, ('row', 'col')), may hold values from -5 to 5
- noise_level: float32 [2], replicated, may hold values from 0.25 to 4
- atom_single: bfloat16 [16384, 128], P(('row', 'col')), may hold values from -21 to 21
- w_pos: float32 [3, 128], replicated, may hold values from -3.5 to 3.5
- atom_bias: bfloat16 [4, 16384, 128], P(None, ('row', 'col')), may hold values from -4 to 250
- atom_qkv: bfloat16 [128, 384], replicated, may hold values from -0.5 to 0.5
- atom_out: bfloat16 [128, 128], replicated, may hold values from -0.5 to 0.5
- w_agg: bfloat16 [128, 768], replicated, may hold values from -0.5 to 0.5
- atom_token: int32 [16384], P(('row', 'col')), may hold values from 0 to 2047, as said below
- token_counts: int32 [2048], P(('row', 'col')), may hold values from 2 to 24, as said below
- pair: bfloat16 [2048, 2048, 128], P('row', 'col'), may hold values from -82 to 82
- w_pairbias: bfloat16 [128, 32], replicated, may hold values from -4 to 4
- tok_proj: bfloat16 [2, 768, 3072], replicated, may hold values from -0.21875 to 0.21875
- tok_out: bfloat16 [2, 768, 768], replicated, may hold values from -0.21875 to 0.21875
- w_dec: bfloat16 [768, 128], replicated, may hold values from -0.21875 to 0.21875
- w_update: bfloat16 [128, 3], replicated, may hold values from -0.5 to 0.5
Outputs:
- denoised: float32 [2, 3, 16384], P(None, None, ('row', 'col'))
The draws below stay inside these ranges and needn't reach their ends.
Inputs may be any that keep to these rules, and one draw needn't show every extreme that they name: `atom_token`: nondecreasing along the atoms; the atoms of device index d along row+col (atoms d*128 to d*128 + 127) belong to tokens (d-1)*16 to (d+1)*16 - 1, those of device 0 to tokens below 16. token_counts[n] is the number of atoms a with atom_token[a] = n.
All inputs are finite; a program needn't handle non-finite values.
Results may differ from the reference program's by a relative error of at most 0.01005.
Values may be sent and summed in bfloat16 or wider, within the bound.
A program may use at most 128 MiB of HBM per device.

```python
import math
import jax
import jax.numpy as jnp
from jax import lax

D_TOK = 768
HEADS = 16
HEAD = 48
C_ATOM = 128
HEADS_A = 4
HEAD_A = 32
C_PAIR = 128
Q_WIN = 32
K_WIN = 128
BLOCKS = 2
SAMPLES = 2
ATOM_RATIO = 8
TOK_DEV = 16
A_DEV = 128
N_TOK = 2048
ATOMS = 16384


def token_starts(key):
    blocks = N_TOK // TOK_DEV
    key_off, key_jit = jax.random.split(key)
    offsets = jax.random.randint(key_off, (blocks,), 0, A_DEV // 2, dtype=jnp.int32)
    block_ids = jnp.arange(blocks, dtype=jnp.int32)
    offsets = jnp.where(block_ids == 0, 0, offsets)
    offsets = jnp.where(block_ids == 1, A_DEV // 2, offsets)
    block_first = block_ids * A_DEV + offsets
    block_next = jnp.concatenate([block_first[1:], jnp.full((1,), ATOMS, dtype=jnp.int32)])
    lengths = block_next - block_first
    spacing = lengths // TOK_DEV
    upper = jnp.broadcast_to(jnp.maximum(spacing - 1, 1)[:, None], (blocks, TOK_DEV))
    jitter = jax.random.randint(key_jit, (blocks, TOK_DEV), 0, upper, dtype=jnp.int32)
    token_slot = jnp.arange(TOK_DEV, dtype=jnp.int32)
    jitter = jnp.where(token_slot[None, :] == 0, 0, jitter)
    starts = block_first[:, None] + token_slot[None, :] * lengths[:, None] // TOK_DEV + jitter
    longest = 3 * ATOM_RATIO
    remaining = A_DEV + A_DEV // 2 - longest
    leading = longest + (token_slot - 1) * remaining // (TOK_DEV - 1)
    leading = jnp.where(token_slot == 0, 0, leading).astype(jnp.int32)
    starts = jnp.where(block_ids[:, None] == 0, leading[None, :], starts)
    return starts.reshape(N_TOK).astype(jnp.int32)


def draw_atom_token(key, part):
    starts = token_starts(key)
    atom_index = jnp.arange(ATOMS, dtype=jnp.int32)
    return (jnp.searchsorted(starts, atom_index, side='right') - 1).astype(jnp.int32)


def draw_token_counts(key, part):
    starts = token_starts(key)
    following = jnp.concatenate([starts[1:], jnp.full((1,), ATOMS, dtype=jnp.int32)])
    return (following - starts).astype(jnp.int32)


def draw_atom_single(key, part):
    key = jax.random.fold_in(key, 5)
    key_row, key_col, key_base = jax.random.split(key, 3)
    row_scale = jnp.exp(jax.random.uniform(key_row, (ATOMS, 1), minval=0.0, maxval=math.log(3.2)))
    col_scale = jnp.exp(jax.random.uniform(key_col, (1, C_ATOM), minval=0.0, maxval=math.log(3.2)))
    base = jnp.clip(jax.random.normal(key_base, (ATOMS, C_ATOM)), -4.0, 4.0)
    return (0.5 * base * row_scale * col_scale).astype(jnp.bfloat16)


def draw_atom_bias(key, part):
    key = jax.random.fold_in(key, 7)
    key_base = jax.random.fold_in(key, 0)
    field = jnp.clip(jax.random.normal(key_base, (HEADS_A, ATOMS, K_WIN)), -4.0, 4.0)
    return field.astype(jnp.bfloat16)


def draw_pair(key, part):
    key = jax.random.fold_in(key, 11)
    key_row, key_col, key_chan, key_base = jax.random.split(key, 4)
    rows_scale = jnp.exp(jax.random.uniform(key_row, (N_TOK, 1, 1), minval=0.0, maxval=math.log(3.2)))
    cols_scale = jnp.exp(jax.random.uniform(key_col, (1, N_TOK, 1), minval=0.0, maxval=math.log(3.2)))
    chan_scale = jnp.exp(jax.random.uniform(key_chan, (1, 1, C_PAIR), minval=0.0, maxval=math.log(2.0)))
    base = jnp.clip(jax.random.normal(key_base, (N_TOK, N_TOK, C_PAIR)), -4.0, 4.0)
    field = base * rows_scale * cols_scale * chan_scale
    return field.astype(jnp.bfloat16)


def draw_w_pairbias(key, part):
    key = jax.random.fold_in(key, 13)
    base = jnp.clip(jax.random.normal(key, (C_PAIR, BLOCKS * HEADS)), -4.0, 4.0) / math.sqrt(C_PAIR)
    return base.astype(jnp.bfloat16)


def block_levels(stream_key, shape, shards, low, largest):
    def one(dim, parts):
        heights = jax.random.uniform(jax.random.fold_in(jax.random.fold_in(stream_key, 6), dim), (parts,), jnp.float32, low / len(shards), largest / len(shards))
        return jnp.repeat(jnp.exp(heights), shape[dim] // parts).reshape((-1,) + (1,) * (len(shape) - dim - 1))

    loudness = one(*shards[0])
    for cut in shards[1:]:
        loudness = loudness * one(*cut)
    return loudness


def gaussian(stream_key, dims, deviation, most, cuts=(), kind=jnp.bfloat16):
    factor_of = block_levels(stream_key, dims, cuts, -0.22, 0.18) if cuts else 1.0
    array = jax.random.normal(stream_key, dims, jnp.float32) * deviation * factor_of
    return jnp.minimum(jnp.maximum(array, -most), most).astype(kind)


def setup_inputs(seed: int = 0) -> dict:
    key_list = jax.random.split(jax.random.key(seed), 18)
    return {
        "atom_pos": gaussian(key_list[0], (SAMPLES, 3, ATOMS), 1.0, 5.0, ((2, 128),), jnp.float32),
        "noise": gaussian(key_list[1], (SAMPLES, 3, ATOMS), 1.0, 5.0, ((2, 128),), jnp.float32),
        "noise_level": jnp.clip(jnp.exp(jax.random.uniform(key_list[2], (SAMPLES,), jnp.float32, math.log(0.25), math.log(4.0))), 0.25, 4.0),
        "atom_single": draw_atom_single(jax.random.fold_in(key_list[17], 71), 0),
        "w_pos": gaussian(key_list[4], (3, C_ATOM), 3 ** -0.5, 3.5, (), jnp.float32),
        "atom_bias": draw_atom_bias(jax.random.fold_in(key_list[17], 71), 0),
        "atom_qkv": gaussian(key_list[6], (C_ATOM, 3 * C_ATOM), C_ATOM ** -0.5, 0.5),
        "atom_out": gaussian(key_list[7], (C_ATOM, C_ATOM), C_ATOM ** -0.5, 0.5),
        "w_agg": gaussian(key_list[8], (C_ATOM, D_TOK), C_ATOM ** -0.5, 0.5),
        "atom_token": draw_atom_token(jax.random.fold_in(key_list[17], 71), 0),
        "token_counts": draw_token_counts(jax.random.fold_in(key_list[17], 71), 0),
        "pair": draw_pair(jax.random.fold_in(key_list[17], 71), 0),
        "w_pairbias": draw_w_pairbias(jax.random.fold_in(key_list[17], 71), 0),
        "tok_proj": gaussian(key_list[13], (BLOCKS, D_TOK, 4 * D_TOK), D_TOK ** -0.5, 0.21875),
        "tok_out": gaussian(key_list[14], (BLOCKS, D_TOK, D_TOK), D_TOK ** -0.5, 0.21875),
        "w_dec": gaussian(key_list[15], (D_TOK, C_ATOM), D_TOK ** -0.5, 0.21875),
        "w_update": gaussian(key_list[16], (C_ATOM, 3), C_ATOM ** -0.5, 0.5),
    }


LN_EPSILON = 1e-05

def layer_norm(inputs):
    average = lax.optimization_barrier(jnp.mean(inputs, axis=-1, keepdims=True))
    centred = inputs - average
    variance = lax.optimization_barrier(jnp.mean(centred * centred, axis=-1, keepdims=True))
    return centred / jnp.sqrt(variance + LN_EPSILON)

def window_attention(queries, key_values, atom_bias):
    samples = queries.shape[0]
    total_atoms = queries.shape[1]
    windows = total_atoms // Q_WIN
    margin = (K_WIN - Q_WIN) // 2
    padded = jnp.pad(key_values, ((0, 0), (margin, margin), (0, 0)))
    pieces = [padded[:, offset * Q_WIN:offset * Q_WIN + total_atoms].reshape(samples, windows, Q_WIN, 2 * C_ATOM) for offset in range(K_WIN // Q_WIN)]
    framed = jnp.concatenate(pieces, axis=2)
    window_keys = framed[..., :C_ATOM].reshape(samples, windows, K_WIN, HEADS_A, HEAD_A).astype(jnp.float32)
    window_values = framed[..., C_ATOM:].reshape(samples, windows, K_WIN, HEADS_A, HEAD_A).astype(jnp.float32)
    window_queries = queries.reshape(samples, windows, Q_WIN, HEADS_A, HEAD_A).astype(jnp.float32)
    scores = jnp.einsum('snqhd,snkhd->shnqk', window_queries, window_keys) / math.sqrt(HEAD_A)
    scores = scores + atom_bias.astype(jnp.float32).reshape(HEADS_A, windows, Q_WIN, K_WIN)[None]
    key_index = jnp.arange(windows, dtype=jnp.int32)[:, None] * Q_WIN - margin + jnp.arange(K_WIN, dtype=jnp.int32)[None, :]
    inside = (key_index >= 0) & (key_index < total_atoms)
    scores = jnp.where(inside[None, None, :, None, :], scores, -1e+30)
    row_top = lax.optimization_barrier(jnp.max(scores, axis=-1, keepdims=True))
    exp_scores = jnp.exp(scores - row_top)
    totals = jnp.transpose(lax.optimization_barrier(jnp.sum(exp_scores, axis=-1)), (0, 2, 3, 1))[..., None]
    weights_low = exp_scores.astype(jnp.bfloat16).astype(jnp.float32)
    mixed = jnp.einsum('shnqk,snkhd->snqhd', weights_low, window_values)
    return (mixed / totals).reshape(samples, total_atoms, C_ATOM).astype(jnp.bfloat16)

def reference(atom_pos, noise, noise_level, atom_single, w_pos, atom_bias, atom_qkv, atom_out, w_agg, atom_token, token_counts, pair, w_pairbias, tok_proj, tok_out, w_dec, w_update):
    noise_scale = noise_level[:, None, None]
    noisy_pos = atom_pos + noise_scale * noise
    scaled = noisy_pos / jnp.sqrt(noise_scale * noise_scale + 1.0)
    atom_act = atom_single.astype(jnp.float32)[None] + jnp.einsum('sca,cd->sad', scaled, w_pos, precision=lax.Precision.HIGHEST)
    atom_norm = layer_norm(atom_act).astype(jnp.bfloat16)
    projected = jnp.einsum('sac,ce->sae', atom_norm.astype(jnp.float32), atom_qkv.astype(jnp.float32)).astype(jnp.bfloat16)
    atom_mix = window_attention(projected[..., :C_ATOM], projected[..., C_ATOM:], atom_bias)
    atom_enc = atom_act + jnp.einsum('sac,ce->sae', atom_mix.astype(jnp.float32), atom_out.astype(jnp.float32))
    encoded_low = atom_enc.astype(jnp.bfloat16)
    hidden = jax.nn.relu(jnp.einsum('sac,cd->sad', encoded_low.astype(jnp.float32), w_agg.astype(jnp.float32)))
    partial_sums = jax.ops.segment_sum(jnp.transpose(hidden, (1, 0, 2)), atom_token, N_TOK)
    token_act = jnp.transpose(partial_sums, (1, 0, 2)) / token_counts.astype(jnp.float32)[None, :, None]
    samples = atom_pos.shape[0]
    group_rows = 128 if N_TOK % 128 == 0 else N_TOK
    groups = N_TOK // group_rows
    for layer_index in range(BLOCKS):
        normed = layer_norm(token_act).astype(jnp.bfloat16)
        token_proj = jnp.einsum('std,de->ste', normed.astype(jnp.float32), tok_proj[layer_index].astype(jnp.float32)).astype(jnp.bfloat16)
        queries_all = token_proj[..., :D_TOK]
        keys_all = token_proj[..., D_TOK:2 * D_TOK].reshape(samples, N_TOK, HEADS, HEAD).astype(jnp.float32)
        values_all = token_proj[..., 2 * D_TOK:3 * D_TOK].reshape(samples, N_TOK, HEADS, HEAD).astype(jnp.float32)
        gates_all = token_proj[..., 3 * D_TOK:]
        bias_weight = w_pairbias[:, layer_index * HEADS:(layer_index + 1) * HEADS].astype(jnp.float32)

        def one_group(group_index):
            first_row = group_index * group_rows
            pair_tile = lax.dynamic_slice_in_dim(pair, first_row, group_rows, 0)
            tile_norm = layer_norm(pair_tile.astype(jnp.float32)).astype(jnp.bfloat16)
            pair_bias = jnp.einsum('rnc,ch->hrn', tile_norm.astype(jnp.float32), bias_weight)
            query_part = lax.dynamic_slice_in_dim(queries_all, first_row, group_rows, 1)
            query_part = query_part.reshape(samples, group_rows, HEADS, HEAD).astype(jnp.float32)
            scores = jnp.einsum('srhd,snhd->shrn', query_part, keys_all) / math.sqrt(HEAD) + pair_bias[None]
            row_top = lax.optimization_barrier(jnp.max(scores, axis=-1, keepdims=True))
            exp_scores = jnp.exp(scores - row_top)
            totals = jnp.transpose(lax.optimization_barrier(jnp.sum(exp_scores, axis=-1)), (0, 2, 1))[..., None]
            weights_low = exp_scores.astype(jnp.bfloat16).astype(jnp.float32)
            mixed = jnp.einsum('shrn,snhd->srhd', weights_low, values_all) / totals
            return mixed.reshape(samples, group_rows, D_TOK)
        attended = lax.map(one_group, jnp.arange(groups, dtype=jnp.int32))
        attended = jnp.transpose(attended, (1, 0, 2, 3)).reshape(samples, N_TOK, D_TOK)
        gated_out = (jax.nn.sigmoid(gates_all.astype(jnp.float32)) * attended).astype(jnp.bfloat16)
        token_act = token_act + jnp.einsum('std,de->ste', gated_out.astype(jnp.float32), tok_out[layer_index].astype(jnp.float32))
    token_decoded = jnp.einsum('std,dc->stc', token_act.astype(jnp.bfloat16).astype(jnp.float32), w_dec.astype(jnp.float32))
    atom_dec = atom_enc + token_decoded[:, atom_token]
    dec_norm = layer_norm(atom_dec).astype(jnp.bfloat16)
    update = jnp.einsum('sac,ce->sea', dec_norm.astype(jnp.float32), w_update.astype(jnp.float32))
    return noisy_pos / (noise_scale * noise_scale + 1.0) + noise_scale / jnp.sqrt(noise_scale * noise_scale + 1.0) * update
```

```python
import math

import jax
import jax.numpy as jnp
from jax import lax
from jax.experimental import pallas as pl
from jax.experimental.pallas import tpu as pltpu
from jax.sharding import PartitionSpec as P

HEADS = 16
HEAD = 48
D_TOK = 768
HEADS_A = 4
HEAD_A = 32
C_ATOM = 128
Q_WIN = 32
K_WIN = 128
MARGIN = 48
BLOCKS = 2
SAMPLES = 2
TOK_DEV = 16
A_DEV = 128
ROWS = 16
COLS = 8
DEVICES = ROWS * COLS
QUERIES = COLS * TOK_DEV
KEYS = ROWS * TOK_DEV
PART = D_TOK + 256
STRIDE = QUERIES + 8
LN_EPSILON = 1e-05
LOG2E = math.log2(math.e)
MESH = pl.DeviceIdType.MESH
F32 = jnp.float32
BF16 = jnp.bfloat16

HEAD_TILES = ((0, 1), (0, 1), (0, 2), (1, 1), (1, 1), (1, 2), (2, 1), (2, 1))


def dot(a, b, dims=((1,), (0,)), precision=None):
    return lax.dot_general(
        a, b, (dims, ((), ())), precision=precision, preferred_element_type=F32
    )


def iota(shape, dim):
    return lax.broadcasted_iota(jnp.int32, shape, dim)


def layer_norm(v):
    mean = jnp.mean(v, axis=-1, keepdims=True)
    centred = v - mean
    var = jnp.mean(centred * centred, axis=-1, keepdims=True)
    return centred * lax.rsqrt(var + LN_EPSILON)


def kernel(
    noise_level,
    atom_pos,
    noise,
    atom_single,
    w_pos,
    atom_bias,
    atom_qkv,
    atom_out,
    w_agg,
    atom_token,
    token_counts,
    pair_hbm,
    w_pairbias,
    tok_proj_hbm,
    tok_out_hbm,
    w_dec,
    w_update,
    out,
    pair,
    proj,
    tok_out,
    bias,
    w_cat,
    centre,
    expand,
    atom_enc,
    queries_a,
    kv_own,
    halo,
    kv_pad,
    spill_out,
    spill_in,
    token_act,
    q_all,
    kv_all,
    q_ref,
    k_ref,
    v_ref,
    stat,
    part,
    part_in,
    dec_out,
    dec_in,
    pair_sem,
    weight_sem,
    halo_send,
    halo_recv,
    spill_sems,
    dec_sems,
    turn_send,
    turn_recv,
    q_send,
    q_recv,
    kv_send,
    kv_recv,
    part_send,
    part_recv,
):
    r = lax.axis_index("row")
    c = lax.axis_index("col")
    d = r * COLS + c
    up = lax.rem(d + 1, DEVICES)
    down = lax.rem(d + DEVICES - 1, DEVICES)
    up_id = (lax.div(up, COLS), lax.rem(up, COLS))
    down_id = (lax.div(down, COLS), lax.rem(down, COLS))
    core = lax.rem(r, 2)
    turn_id = (2 * c + core, lax.div(r, 2))
    own = turn_id[0] == r
    slot = core * COLS + lax.div(r, 2)
    turn_slot = core * COLS + c

    def pair_copy(i):
        rows = pl.ds(i * 32, 32)
        return pltpu.make_async_copy(pair_hbm.at[rows], pair.at[rows], pair_sem.at[i])

    weight_copies = (
        [pltpu.make_async_copy(tok_proj_hbm.at[b], proj.at[b], weight_sem.at[b]) for b in range(2)]
        + [pltpu.make_async_copy(tok_out_hbm.at[b], tok_out.at[b], weight_sem.at[2 + b]) for b in range(2)]
    )
    for i in range(4):
        pair_copy(i).start()
    for i in (0, 2, 1, 3):
        weight_copies[i].start()

    barrier = pltpu.get_barrier_semaphore()

    def greet_col(j, _):
        pl.semaphore_signal(
            barrier, inc=1, device_id=(r, lax.rem(c + j, COLS)), device_id_type=MESH
        )
        return 0

    def greet_row(j, _):
        pl.semaphore_signal(
            barrier, inc=1, device_id=(lax.rem(r + j, ROWS), c), device_id_type=MESH
        )
        return 0

    lax.fori_loop(1, COLS, greet_col, 0)
    lax.fori_loop(1, ROWS, greet_row, 0)
    pl.semaphore_signal(barrier, inc=1, device_id=up_id, device_id_type=MESH)
    pl.semaphore_signal(barrier, inc=1, device_id=down_id, device_id_type=MESH)

    @pl.when(jnp.logical_not(own))
    def _():
        pl.semaphore_signal(barrier, inc=1, device_id=turn_id, device_id_type=MESH)

    row_i, col_i = iota((C_ATOM, C_ATOM), 0), iota((C_ATOM, C_ATOM), 1)
    centre[...] = (
        jnp.where(row_i == col_i, 1.0, 0.0) - 1.0 / C_ATOM
    ).astype(BF16)
    wide = jnp.concatenate(
        [w_pairbias[...].astype(F32), jnp.zeros((C_ATOM, C_ATOM - 2 * HEADS), F32)], axis=1
    )
    w_cat[...] = jnp.zeros_like(w_cat)
    w_cat[0 : 2 * HEADS, 0:C_ATOM] = wide.T[0 : 2 * HEADS].astype(BF16)
    w_cat[2 * HEADS : 2 * HEADS + 16, C_ATOM : 2 * C_ATOM] = jnp.ones((16, C_ATOM), BF16)

    def pair_bias(first, count):
        unroll = 4

        def step(i, _):
            for u in range(unroll):
                q = first + i * unroll + u
                centred = dot(pair[q], centre[...])
                both = jnp.concatenate(
                    [centred.astype(BF16), (centred * centred).astype(BF16)], axis=1
                )
                y = dot(w_cat[...], both, ((1,), (1,)))
                scale = lax.rsqrt(y[32:40] * (1.0 / C_ATOM) + LN_EPSILON) * LOG2E
                scaled_y = (y[0:32].reshape(4, 8, KEYS) * scale[None]).reshape(2 * HEADS, KEYS)
                for t in range(KEYS // 128):
                    bias[t, pl.ds(q, 2 * HEADS, stride=STRIDE), :] = scaled_y[
                        :, t * 128 : (t + 1) * 128
                    ]
            return 0

        lax.fori_loop(0, count // unroll, step, 0)

    acts = []
    for s in range(SAMPLES):
        level = jnp.full((1, A_DEV), noise_level[s], F32)
        noisy = atom_pos[s] + level * noise[s]
        scaled = noisy / jnp.sqrt(level * level + 1.0)
        acts.append(
            atom_single[...].astype(F32)
            + dot(scaled, w_pos[...], ((0,), (0,)), lax.Precision.HIGHEST)
        )
    act = jnp.concatenate(acts, axis=0)
    atom_enc[...] = act
    projected = dot(layer_norm(act).astype(BF16), atom_qkv[...]).astype(BF16)
    for s in range(SAMPLES):
        rows = slice(s * A_DEV, (s + 1) * A_DEV)
        queries_a[s] = projected[rows, 0:C_ATOM]
        kv_own[s] = projected[rows, C_ATOM:]
    pl.semaphore_wait(barrier, 2 + (COLS - 1) + (ROWS - 1) + jnp.where(own, 0, 1))

    def halo_copies():
        return (
            pltpu.make_async_remote_copy(
                src_ref=kv_own.at[:, pl.ds(A_DEV - MARGIN, MARGIN)],
                dst_ref=halo.at[0],
                send_sem=halo_send.at[0],
                recv_sem=halo_recv.at[0],
                device_id=up_id,
                device_id_type=MESH,
            ),
            pltpu.make_async_remote_copy(
                src_ref=kv_own.at[:, pl.ds(0, MARGIN)],
                dst_ref=halo.at[1],
                send_sem=halo_send.at[1],
                recv_sem=halo_recv.at[1],
                device_id=down_id,
                device_id_type=MESH,
            ),
        )

    to_up, to_down = halo_copies()
    to_up.start()
    to_down.start()
    for i in range(4):
        pair_copy(i).wait()
    pair_bias(0, 32)
    to_up.wait()
    to_down.wait()
    for s in range(SAMPLES):
        kv_pad[s, 0:MARGIN] = halo[0, s]
        kv_pad[s, MARGIN : MARGIN + A_DEV] = kv_own[s]
        kv_pad[s, MARGIN + A_DEV : A_DEV + 2 * MARGIN] = halo[1, s]

    lane_head = iota((HEADS_A, Q_WIN, C_ATOM), 2) // HEAD_A == iota((HEADS_A, Q_WIN, C_ATOM), 0)
    head_mask = jnp.where(lane_head, 1.0, 0.0)
    head_mask_low = head_mask.astype(BF16)
    slots = iota((1, K_WIN), 1)
    for s in range(SAMPLES):
        mixed = []
        for w in range(A_DEV // Q_WIN):
            rows = slice(w * Q_WIN, (w + 1) * Q_WIN)
            window = slice(w * Q_WIN, w * Q_WIN + K_WIN)
            query = (queries_a[s, rows][None] * head_mask_low).reshape(HEADS_A * Q_WIN, C_ATOM)
            score = dot(query, kv_pad[s, window, 0:C_ATOM], ((1,), (1,))) * (1 / math.sqrt(HEAD_A))
            score = score + atom_bias[:, rows, :].astype(F32).reshape(HEADS_A * Q_WIN, K_WIN)
            index = d * A_DEV + w * Q_WIN - MARGIN + slots
            inside = (index >= 0) & (index < DEVICES * A_DEV)
            score = jnp.where(inside, score, -1e30)
            p = jnp.exp(score - jnp.max(score, axis=-1, keepdims=True))
            total = jnp.sum(p, axis=-1, keepdims=True)
            mix = dot(p.astype(BF16), kv_pad[s, window, C_ATOM:]) / total
            mixed.append(
                jnp.sum(mix.reshape(HEADS_A, Q_WIN, C_ATOM) * head_mask, axis=0)
            )
        rows = slice(s * A_DEV, (s + 1) * A_DEV)
        mix = jnp.concatenate(mixed, axis=0).astype(BF16)
        atom_enc[rows] = atom_enc[rows] + dot(mix, atom_out[...])

    slot_index = atom_token[...] - (d * TOK_DEV - TOK_DEV)
    member = jnp.where(
        slot_index == iota((2 * TOK_DEV, A_DEV), 0), 1.0, 0.0
    )
    member_low = member.astype(BF16)
    hidden = jnp.maximum(dot(atom_enc[...].astype(BF16), w_agg[...]), 0.0)
    for s in range(SAMPLES):
        mine = hidden[s * A_DEV : (s + 1) * A_DEV]
        high = mine.astype(BF16)
        low = (mine - high.astype(F32)).astype(BF16)
        sums = dot(
            jnp.concatenate([member_low, member_low], axis=1),
            jnp.concatenate([high, low], axis=0),
        )
        spill_out[s] = sums[0:TOK_DEV].astype(BF16)
        token_act[s] = sums[TOK_DEV : 2 * TOK_DEV]
    spill = pltpu.make_async_remote_copy(
        src_ref=spill_out,
        dst_ref=spill_in,
        send_sem=spill_sems.at[0],
        recv_sem=spill_sems.at[1],
        device_id=down_id,
        device_id_type=MESH,
    )
    spill.start()
    pair_bias(32, 32)
    lanes = iota((D_TOK, 2 * C_ATOM), 0)
    head_of = lax.rem(iota((D_TOK, 2 * C_ATOM), 1), C_ATOM)
    expand[...] = jnp.where(
        (lanes >= head_of * HEAD) & (lanes < head_of * HEAD + HEAD), 1.0, 0.0
    ).astype(BF16)
    diagonal = iota((TOK_DEV, TOK_DEV), 0) == iota((TOK_DEV, TOK_DEV), 1)
    counts = jnp.sum(
        jnp.where(diagonal, token_counts[...].astype(F32), 0.0), axis=1, keepdims=True
    )
    spill.wait()
    for s in range(SAMPLES):
        token_act[s] = (token_act[s] + spill_in[s].astype(F32)) / counts

    def q_copy(b, s, j):
        return pltpu.make_async_remote_copy(
            src_ref=q_all.at[b, s, c],
            dst_ref=q_all.at[b, s, c],
            send_sem=q_send.at[b, s, j],
            recv_sem=q_recv.at[b, s, c],
            device_id=(r, lax.rem(c + j, COLS)),
            device_id_type=MESH,
        )

    def q_arrival(b, s, j):
        peer = lax.rem(c + j, COLS)
        return pltpu.make_async_remote_copy(
            src_ref=q_all.at[b, s, peer],
            dst_ref=q_all.at[b, s, peer],
            send_sem=q_send.at[b, s, j],
            recv_sem=q_recv.at[b, s, peer],
            device_id=(r, peer),
            device_id_type=MESH,
        )

    def turn_copy(b, s):
        return pltpu.make_async_remote_copy(
            src_ref=q_all.at[b, s, c],
            dst_ref=kv_all.at[b, s, turn_slot],
            send_sem=turn_send.at[b, s],
            recv_sem=turn_recv.at[b, s],
            device_id=turn_id,
            device_id_type=MESH,
        )

    def turn_arrival(b, s):
        return pltpu.make_async_remote_copy(
            src_ref=q_all.at[b, s, c],
            dst_ref=kv_all.at[b, s, slot],
            send_sem=turn_send.at[b, s],
            recv_sem=turn_recv.at[b, s],
            device_id=turn_id,
            device_id_type=MESH,
        )

    def kv_copy(b, s, j):
        return pltpu.make_async_remote_copy(
            src_ref=kv_all.at[b, s, slot],
            dst_ref=kv_all.at[b, s, slot],
            send_sem=kv_send.at[b, s, j],
            recv_sem=kv_recv.at[b, s, slot],
            device_id=(lax.rem(r + j, ROWS), c),
            device_id_type=MESH,
        )

    def kv_arrival(b, s, j):
        peer = lax.rem(r + j, ROWS)
        peer_slot = lax.rem(peer, 2) * COLS + lax.div(peer, 2)
        return pltpu.make_async_remote_copy(
            src_ref=kv_all.at[b, s, peer_slot],
            dst_ref=kv_all.at[b, s, peer_slot],
            send_sem=kv_send.at[b, s, j],
            recv_sem=kv_recv.at[b, s, peer_slot],
            device_id=(peer, c),
            device_id_type=MESH,
        )

    def part_copy(b, s, j):
        peer = lax.rem(c + j, COLS)
        return pltpu.make_async_remote_copy(
            src_ref=part.at[b, s, peer],
            dst_ref=part_in.at[b, s, c],
            send_sem=part_send.at[b, s, j],
            recv_sem=part_recv.at[b, s, c],
            device_id=(r, peer),
            device_id_type=MESH,
        )

    def part_arrival(b, s, j):
        peer = lax.rem(c + j, COLS)
        return pltpu.make_async_remote_copy(
            src_ref=part.at[b, s, peer],
            dst_ref=part_in.at[b, s, peer],
            send_sem=part_send.at[b, s, j],
            recv_sem=part_recv.at[b, s, peer],
            device_id=(r, peer),
            device_id_type=MESH,
        )

    def each(first, last, act):
        def step(j, _):
            act(j)
            return 0

        lax.fori_loop(first, last, step, 0)

    def send_normed(b, s):
        normed = layer_norm(token_act[s]).astype(BF16)
        q_all[b, s, c] = normed

        @pl.when(own)
        def _():
            kv_all[b, s, slot] = normed

        @pl.when(jnp.logical_not(own))
        def _():
            turn_copy(b, s).start()

        each(1, COLS, lambda j: q_copy(b, s, j).start())

    def pass_on(b, s):
        @pl.when(jnp.logical_not(own))
        def _():
            turn_arrival(b, s).wait_recv()

        each(1, ROWS, lambda j: kv_copy(b, s, j).start())

    def attention(b, s):
        each(1, COLS, lambda j: q_arrival(b, s, j).wait_recv())
        normed_rows = q_all[b, s].reshape(QUERIES, D_TOK)
        for n in range(0, D_TOK, 256):
            q_ref[:, n : n + 256] = dot(normed_rows, proj[b, :, n : n + 256]).astype(BF16)
        each(1, ROWS, lambda j: kv_arrival(b, s, j).wait_recv())
        normed_keys = kv_all[b, s].reshape(KEYS, D_TOK)
        for n in range(0, D_TOK, 256):
            k_ref[:, n : n + 256] = dot(
                normed_keys, proj[b, :, D_TOK + n : D_TOK + n + 256]
            ).astype(BF16)
            v_ref[:, n : n + 256] = dot(
                normed_keys, proj[b, :, 2 * D_TOK + n : 2 * D_TOK + n + 256]
            ).astype(BF16)
        stat[...] = jnp.zeros_like(stat)
        lane = iota((QUERIES, C_ATOM), 1)

        def group(g, _):
            base = g * (8 * HEAD)
            outs = []
            stats = stat[...]
            for hh, (tile, tiles) in enumerate(HEAD_TILES):
                window = pl.ds(pl.multiple_of(base + tile * 128, 128), tiles * 128)
                at = iota((QUERIES, tiles * 128), 1) + tile * 128
                mine = (at >= hh * HEAD) & (at < (hh + 1) * HEAD)
                query = q_ref[:, window] * jnp.where(mine, 1.0, 0.0).astype(BF16)
                rows = pl.ds(pl.multiple_of((b * HEADS + g * 8 + hh) * STRIDE, 8), QUERIES)
                score = dot(query, k_ref[:, window], ((1,), (1,))) * (
                    LOG2E / math.sqrt(HEAD)
                ) + jnp.concatenate([bias[t, rows, :] for t in range(KEYS // 128)], axis=1)
                top = jnp.max(score, axis=-1, keepdims=True)
                top_high = top.astype(BF16).astype(F32)
                top = top_high + (top - top_high).astype(BF16).astype(F32)
                p = jnp.exp2(score - top)
                total = jnp.sum(p, axis=-1, keepdims=True)
                outs.append(dot(p.astype(BF16), v_ref[:, window]))
                stats = jnp.where(lane == g * 8 + hh, top, stats)
                stats = jnp.where(lane == HEADS + g * 8 + hh, total, stats)
            stat[...] = stats
            o0, o1, o2, o3, o4, o5, o6, o7 = outs
            tiles = (
                jnp.where(lane < 48, o0, jnp.where(lane < 96, o1, o2[:, :128])),
                jnp.where(
                    lane < 16,
                    o2[:, 128:],
                    jnp.where(lane < 64, o3, jnp.where(lane < 112, o4, o5[:, :128])),
                ),
                jnp.where(lane < 32, o5[:, 128:], jnp.where(lane < 80, o6, o7)),
            )
            for t, value in enumerate(tiles):
                where = pl.ds(pl.multiple_of(base + t * 128, 128), 128)
                part[b, s, :, :, where] = value.astype(BF16).reshape(COLS, TOK_DEV, 128)
            return 0

        lax.fori_loop(0, 2, group, 0)
        high = stat[...].astype(BF16)
        low = (stat[...] - high.astype(F32)).astype(BF16)
        part[b, s, :, :, D_TOK : D_TOK + 128] = high.reshape(COLS, TOK_DEV, 128)
        part[b, s, :, :, D_TOK + 128 : PART] = low.reshape(COLS, TOK_DEV, 128)
        each(1, COLS, lambda j: part_copy(b, s, j).start())
        part_in[b, s, c] = part[b, s, c]

    def combine(b, s):
        gate = dot(q_all[b, s, c], proj[b, :, 3 * D_TOK :]).astype(BF16).astype(F32)
        gate = 1.0 / (1.0 + jnp.exp(-gate))
        each(1, COLS, lambda j: part_arrival(b, s, j).wait_recv())
        stats = part_in[b, s, :, :, D_TOK : D_TOK + 128].astype(F32) + part_in[
            b, s, :, :, D_TOK + 128 : PART
        ].astype(F32)
        weight = jnp.exp2(stats - jnp.max(stats, axis=0, keepdims=True))
        dens = pltpu.roll(stats.reshape(QUERIES, 128), 128 - HEADS, 1).reshape(stats.shape)
        total = jnp.sum(weight * dens, axis=0, keepdims=True)
        weight = jnp.where(iota(stats.shape, 2) < HEADS, weight / total, 0.0)
        weight = weight.reshape(QUERIES, 128)
        high = weight.astype(BF16)
        low = (weight - high.astype(F32)).astype(BF16)
        spread = dot(jnp.concatenate([high, low], axis=1), expand[...], ((1,), (1,)))
        nums = part_in[b, s, :, :, 0:D_TOK].astype(F32)
        mix = jnp.sum(nums * spread.reshape(COLS, TOK_DEV, D_TOK), axis=0)
        gated = (gate * mix).astype(BF16)
        token_act[s] = token_act[s] + dot(gated, tok_out[b])

    for s in range(SAMPLES):
        send_normed(0, s)
    pair_bias(64, 32)
    for s in range(SAMPLES):
        pass_on(0, s)
    pair_bias(96, 32)
    for copy in weight_copies:
        copy.wait()
    for s in range(SAMPLES):
        attention(0, s)
    for s in range(SAMPLES):
        combine(0, s)
        send_normed(1, s)
    for s in range(SAMPLES):
        pass_on(1, s)
    for s in range(SAMPLES):
        attention(1, s)
    for s in range(SAMPLES):
        combine(1, s)

    for s in range(SAMPLES):
        dec_out[s] = dot(token_act[s].astype(BF16), w_dec[...])
    decoded = pltpu.make_async_remote_copy(
        src_ref=dec_out,
        dst_ref=dec_in,
        send_sem=dec_sems.at[0],
        recv_sem=dec_sems.at[1],
        device_id=up_id,
        device_id_type=MESH,
    )
    decoded.start()
    for b in range(BLOCKS):
        for s in range(SAMPLES):
            each(1, COLS, lambda j: q_copy(b, s, j).wait_send())
            each(1, ROWS, lambda j: kv_copy(b, s, j).wait_send())
            each(1, COLS, lambda j: part_copy(b, s, j).wait_send())

            @pl.when(jnp.logical_not(own))
            def _():
                turn_copy(b, s).wait_send()

    decoded.wait()
    member3 = jnp.concatenate([member_low] * 3, axis=0)
    for s in range(SAMPLES):
        table = jnp.concatenate([dec_in[s], dec_out[s]], axis=0)
        high = table.astype(BF16)
        rest = table - high.astype(F32)
        mid = rest.astype(BF16)
        low = (rest - mid.astype(F32)).astype(BF16)
        picked = dot(member3, jnp.concatenate([high, mid, low], axis=0), ((0,), (0,)))
        atom_dec = atom_enc[s * A_DEV : (s + 1) * A_DEV] + picked
        update = dot(w_update[...], layer_norm(atom_dec).astype(BF16), ((0,), (1,)))
        level = jnp.full((1, A_DEV), noise_level[s], F32)
        noisy = atom_pos[s] + level * noise[s]
        square = level * level + 1.0
        out[s] = noisy / square + level / jnp.sqrt(square) * update


def body(
    atom_pos,
    noise,
    noise_level,
    atom_single,
    w_pos,
    atom_bias,
    atom_qkv,
    atom_out,
    w_agg,
    atom_token,
    token_counts,
    pair,
    w_pairbias,
    tok_proj,
    tok_out,
    w_dec,
    w_update,
):
    vmem = pl.BlockSpec(memory_space=pltpu.VMEM)
    hbm = pl.BlockSpec(memory_space=pl.ANY)
    dma = pltpu.SemaphoreType.DMA
    return pl.pallas_call(
        kernel,
        out_shape=jax.ShapeDtypeStruct((SAMPLES, 3, A_DEV), F32),
        in_specs=[pl.BlockSpec(memory_space=pltpu.SMEM)]
        + [vmem] * 10
        + [hbm, vmem, hbm, hbm, vmem, vmem],
        out_specs=vmem,
        scratch_shapes=[
            pltpu.VMEM((QUERIES, KEYS, C_ATOM), BF16),
            pltpu.VMEM((BLOCKS, D_TOK, 4 * D_TOK), BF16),
            pltpu.VMEM((BLOCKS, D_TOK, D_TOK), BF16),
            pltpu.VMEM((KEYS // 128, 2 * HEADS * STRIDE, 128), F32),
            pltpu.VMEM((2 * HEADS + 16, 2 * C_ATOM), BF16),
            pltpu.VMEM((C_ATOM, C_ATOM), BF16),
            pltpu.VMEM((D_TOK, 2 * C_ATOM), BF16),
            pltpu.VMEM((SAMPLES * A_DEV, C_ATOM), F32),
            pltpu.VMEM((SAMPLES, A_DEV, C_ATOM), BF16),
            pltpu.VMEM((SAMPLES, A_DEV, 2 * C_ATOM), BF16),
            pltpu.VMEM((2, SAMPLES, MARGIN, 2 * C_ATOM), BF16),
            pltpu.VMEM((SAMPLES, A_DEV + 2 * MARGIN, 2 * C_ATOM), BF16),
            pltpu.VMEM((SAMPLES, TOK_DEV, D_TOK), BF16),
            pltpu.VMEM((SAMPLES, TOK_DEV, D_TOK), BF16),
            pltpu.VMEM((SAMPLES, TOK_DEV, D_TOK), F32),
            pltpu.VMEM((BLOCKS, SAMPLES, COLS, TOK_DEV, D_TOK), BF16),
            pltpu.VMEM((BLOCKS, SAMPLES, ROWS, TOK_DEV, D_TOK), BF16),
            pltpu.VMEM((QUERIES, D_TOK), BF16),
            pltpu.VMEM((KEYS, D_TOK), BF16),
            pltpu.VMEM((KEYS, D_TOK), BF16),
            pltpu.VMEM((QUERIES, 128), F32),
            pltpu.VMEM((BLOCKS, SAMPLES, COLS, TOK_DEV, PART), BF16),
            pltpu.VMEM((BLOCKS, SAMPLES, COLS, TOK_DEV, PART), BF16),
            pltpu.VMEM((SAMPLES, TOK_DEV, C_ATOM), F32),
            pltpu.VMEM((SAMPLES, TOK_DEV, C_ATOM), F32),
            dma((4,)),
            dma((4,)),
            dma((2,)),
            dma((2,)),
            dma((2,)),
            dma((2,)),
            dma((BLOCKS, SAMPLES)),
            dma((BLOCKS, SAMPLES)),
            dma((BLOCKS, SAMPLES, COLS)),
            dma((BLOCKS, SAMPLES, COLS)),
            dma((BLOCKS, SAMPLES, ROWS)),
            dma((BLOCKS, SAMPLES, ROWS)),
            dma((BLOCKS, SAMPLES, COLS)),
            dma((BLOCKS, SAMPLES, COLS)),
        ],
        compiler_params=pltpu.CompilerParams(
            collective_id=0, has_side_effects=True, vmem_limit_bytes=56 * 1024 * 1024
        ),
    )(
        noise_level,
        atom_pos,
        noise,
        atom_single,
        w_pos,
        atom_bias,
        atom_qkv,
        atom_out,
        w_agg,
        atom_token.reshape(1, A_DEV),
        token_counts.reshape(1, TOK_DEV),
        pair,
        w_pairbias,
        tok_proj,
        tok_out,
        w_dec,
        w_update,
    )


def solution(mesh):
    return jax.shard_map(
        body,
        mesh=mesh,
        in_specs=(
            P(None, None, ("row", "col")),
            P(None, None, ("row", "col")),
            P(),
            P(("row", "col"), None),
            P(),
            P(None, ("row", "col"), None),
            P(),
            P(),
            P(),
            P(("row", "col")),
            P(("row", "col")),
            P("row", "col", None),
            P(),
            P(),
            P(),
            P(),
            P(),
        ),
        out_specs=P(None, None, ("row", "col")),
        check_vma=False,
    )
```

```python
import math

import jax
import jax.numpy as jnp
from jax import lax
from jax.experimental import pallas as pl
from jax.experimental.pallas import tpu as pltpu
from jax.sharding import PartitionSpec as P

HEADS = 16
HEAD = 48
D_TOK = 768
HEADS_A = 4
HEAD_A = 32
C_ATOM = 128
Q_WIN = 32
K_WIN = 128
MARGIN = 48
BLOCKS = 2
SAMPLES = 2
TOK_DEV = 16
A_DEV = 128
ROWS = 16
COLS = 8
DEVICES = ROWS * COLS
QUERIES = COLS * TOK_DEV
KEYS = ROWS * TOK_DEV
PART = D_TOK + 128
STRIDE = QUERIES + 8
LN_EPSILON = 1e-05
LOG2E = math.log2(math.e)
MESH = pl.DeviceIdType.MESH
F32 = jnp.float32
BF16 = jnp.bfloat16

HEAD_TILES = ((0, 1), (0, 1), (0, 2), (1, 1), (1, 1), (1, 2), (2, 1), (2, 1))


def dot(a, b, dims=((1,), (0,)), precision=None):
    return lax.dot_general(
        a, b, (dims, ((), ())), precision=precision, preferred_element_type=F32
    )


def iota(shape, dim):
    return lax.broadcasted_iota(jnp.int32, shape, dim)


def layer_norm(v):
    mean = jnp.mean(v, axis=-1, keepdims=True)
    centred = v - mean
    var = jnp.mean(centred * centred, axis=-1, keepdims=True)
    return centred * lax.rsqrt(var + LN_EPSILON)


def swap2(i):
    return i + 2 - 4 * lax.rem(lax.div(i, 2), 2)


def kernel(
    noise_level_hbm,
    atom_pos_hbm,
    noise_hbm,
    atom_single_hbm,
    w_pos_hbm,
    atom_bias_hbm,
    atom_qkv_hbm,
    atom_out_hbm,
    w_agg_hbm,
    atom_token_hbm,
    token_counts_hbm,
    pair_hbm,
    w_pairbias_hbm,
    tok_proj_hbm,
    tok_out_hbm,
    w_dec_hbm,
    w_update_hbm,
    out,
    noise_level,
    atom_pos,
    noise,
    atom_single,
    w_pos,
    atom_bias,
    atom_qkv,
    atom_out,
    w_agg,
    atom_token,
    token_counts,
    w_pairbias,
    w_dec,
    w_update,
    pair,
    proj,
    tok_out,
    bias,
    w_spread,
    centre,
    expand,
    atom_enc,
    queries_a,
    kv_own,
    halo,
    kv_pad,
    spill_out,
    spill_in,
    token_act,
    gates,
    q_all,
    kv_all,
    q_ref,
    k_ref,
    v_ref,
    stat,
    part,
    part_in,
    dec_out,
    dec_in,
    input_sem,
    pair_sem,
    weight_sem,
    halo_send,
    halo_recv,
    spill_sems,
    dec_sems,
    turn_send,
    turn_recv,
    q_send,
    q_recv,
    kv_send,
    kv_recv,
    twin_send,
    twin_recv,
    part_send,
    part_recv,
):
    r = lax.axis_index("row")
    c = lax.axis_index("col")
    d = r * COLS + c
    up = lax.rem(d + 1, DEVICES)
    down = lax.rem(d + DEVICES - 1, DEVICES)
    up_id = (lax.div(up, COLS), lax.rem(up, COLS))
    down_id = (lax.div(down, COLS), lax.rem(down, COLS))
    core = lax.rem(r, 2)
    level_r = lax.div(r, 2)
    twin_id = (r + 1 - 2 * core, c)
    turn_to = (2 * swap2(c) + core, level_r)
    turn_from = (2 * c + core, swap2(level_r))
    slot = core * COLS + swap2(level_r)
    turn_slot = core * COLS + c

    barrier = pltpu.get_barrier_semaphore()

    def greet(device):
        pl.semaphore_signal(barrier, inc=1, device_id=device, device_id_type=MESH)

    def each(first, last, act):
        def step(j, _):
            act(j)
            return 0

        lax.fori_loop(first, last, step, 0)

    greet(turn_from)
    greet(up_id)
    greet(down_id)
    each(1, COLS, lambda j: greet((r, lax.rem(c + j, COLS))))
    each(1, ROWS // 2, lambda j: greet((lax.rem(r + 2 * j, ROWS), c)))
    greet(twin_id)

    small = [
        (noise_level_hbm, noise_level),
        (atom_pos_hbm, atom_pos),
        (noise_hbm, noise),
        (atom_single_hbm, atom_single),
        (w_pos_hbm, w_pos),
        (atom_qkv_hbm, atom_qkv),
        (w_pairbias_hbm, w_pairbias),
        (atom_bias_hbm, atom_bias),
        (atom_out_hbm, atom_out),
        (w_agg_hbm, w_agg),
        (atom_token_hbm, atom_token),
        (token_counts_hbm, token_counts),
        (w_dec_hbm, w_dec),
        (w_update_hbm, w_update),
    ]
    small_copies = [
        pltpu.make_async_copy(a, b, input_sem.at[i]) for i, (a, b) in enumerate(small)
    ]
    for copy in small_copies:
        copy.start()

    def pair_copy(i):
        rows = pl.ds(i * 32, 32)
        return pltpu.make_async_copy(pair_hbm.at[rows], pair.at[rows], pair_sem.at[i])

    proj_copies = [
        pltpu.make_async_copy(tok_proj_hbm.at[b], proj.at[b], weight_sem.at[b]) for b in range(2)
    ]
    out_copies = [
        pltpu.make_async_copy(tok_out_hbm.at[b], tok_out.at[b], weight_sem.at[2 + b])
        for b in range(2)
    ]
    for i in range(4):
        pair_copy(i).start()
    for b in range(2):
        proj_copies[b].start()
        out_copies[b].start()
    for copy in small_copies[:7]:
        copy.wait()

    row_i, col_i = iota((KEYS, KEYS), 0), iota((KEYS, KEYS), 1)
    same = row_i // C_ATOM == col_i // C_ATOM
    centre[...] = (
        jnp.where(row_i == col_i, 1.0, 0.0) - jnp.where(same, 1.0 / C_ATOM, 0.0)
    ).astype(BF16)
    heads_wide = iota((2 * HEADS, KEYS), 1) // 8 == iota((2 * HEADS, KEYS), 0)
    wide = dot(w_pairbias[...], jnp.where(heads_wide, 1.0, 0.0).astype(BF16), ((0,), (0,)))
    query_of = lax.rem(iota((C_ATOM, KEYS), 1), 8)
    for q in range(8):
        w_spread[q * C_ATOM : (q + 1) * C_ATOM, :] = jnp.where(query_of == q, wide, 0.0).astype(
            BF16
        )

    def pair_bias(first, last):
        def step(i, _):
            q0 = pl.multiple_of(i * 8, 8)
            centred, squares = [], []
            for p in range(4):
                two = jnp.concatenate([pair[q0 + 2 * p], pair[q0 + 2 * p + 1]], axis=1)
                part_centred = dot(two, centre[...])
                centred.append(part_centred.astype(BF16))
                squares.append(part_centred * part_centred)
            y = dot(jnp.concatenate(centred, axis=1), w_spread[...])
            query = lax.rem(iota((KEYS, C_ATOM), 1), 8)
            total = jnp.zeros((KEYS, C_ATOM), F32)
            for q in range(8):
                half = slice((q % 2) * C_ATOM, (q % 2 + 1) * C_ATOM)
                mine = jnp.sum(squares[q // 2][:, half], axis=1, keepdims=True)
                total = jnp.where(query == q, mine, total)
            scale = lax.rsqrt(total * (1.0 / C_ATOM) + LN_EPSILON) * LOG2E
            turned = (y * jnp.concatenate([scale, scale], axis=1)).T
            for t in range(KEYS // 128):
                for h in range(2 * HEADS):
                    bias[t, pl.ds(pl.multiple_of(h * STRIDE + q0, 8), 8), :] = turned[
                        h * 8 : (h + 1) * 8, t * 128 : (t + 1) * 128
                    ]
            return 0

        lax.fori_loop(first, last, step, 0)

    acts = []
    for s in range(SAMPLES):
        level = jnp.broadcast_to(noise_level[:, s : s + 1], (1, A_DEV))
        noisy = atom_pos[:, s] + level * noise[:, s]
        scaled = noisy / jnp.sqrt(level * level + 1.0)
        acts.append(
            atom_single[...].astype(F32)
            + dot(scaled, w_pos[...], ((0,), (0,)), lax.Precision.HIGHEST)
        )
    act = jnp.concatenate(acts, axis=0)
    atom_enc[...] = act
    projected = dot(layer_norm(act).astype(BF16), atom_qkv[...]).astype(BF16)
    for s in range(SAMPLES):
        rows = slice(s * A_DEV, (s + 1) * A_DEV)
        queries_a[s] = projected[rows, 0:C_ATOM]
        kv_own[s] = projected[rows, C_ATOM:]
    pl.semaphore_wait(barrier, 1 + 2 + (COLS - 1) + (ROWS // 2 - 1) + 1)

    def halo_copies():
        return (
            pltpu.make_async_remote_copy(
                src_ref=kv_own.at[:, pl.ds(A_DEV - MARGIN, MARGIN)],
                dst_ref=halo.at[0],
                send_sem=halo_send.at[0],
                recv_sem=halo_recv.at[0],
                device_id=up_id,
                device_id_type=MESH,
            ),
            pltpu.make_async_remote_copy(
                src_ref=kv_own.at[:, pl.ds(0, MARGIN)],
                dst_ref=halo.at[1],
                send_sem=halo_send.at[1],
                recv_sem=halo_recv.at[1],
                device_id=down_id,
                device_id_type=MESH,
            ),
        )

    to_up, to_down = halo_copies()
    to_up.start()
    to_down.start()
    for i in range(4):
        pair_copy(i).wait()
    pair_bias(0, 6)
    for copy in small_copies[7:]:
        copy.wait()
    to_up.wait()
    to_down.wait()
    for s in range(SAMPLES):
        kv_pad[s, 0:MARGIN] = halo[0, s]
        kv_pad[s, MARGIN : MARGIN + A_DEV] = kv_own[s]
        kv_pad[s, MARGIN + A_DEV : A_DEV + 2 * MARGIN] = halo[1, s]

    lane_head = iota((HEADS_A, Q_WIN, C_ATOM), 2) // HEAD_A == iota((HEADS_A, Q_WIN, C_ATOM), 0)
    head_mask = jnp.where(lane_head, 1.0, 0.0)
    head_mask_low = head_mask.astype(BF16)
    slots = iota((1, K_WIN), 1)
    for s in range(SAMPLES):
        mixed = []
        for w in range(A_DEV // Q_WIN):
            rows = slice(w * Q_WIN, (w + 1) * Q_WIN)
            window = slice(w * Q_WIN, w * Q_WIN + K_WIN)
            query = (queries_a[s, rows][None] * head_mask_low).reshape(HEADS_A * Q_WIN, C_ATOM)
            score = dot(query, kv_pad[s, window, 0:C_ATOM], ((1,), (1,))) * (1 / math.sqrt(HEAD_A))
            score = score + atom_bias[:, rows, :].astype(F32).reshape(HEADS_A * Q_WIN, K_WIN)
            index = d * A_DEV + w * Q_WIN - MARGIN + slots
            inside = (index >= 0) & (index < DEVICES * A_DEV)
            score = jnp.where(inside, score, -1e30)
            p = jnp.exp(score - jnp.max(score, axis=-1, keepdims=True))
            total = jnp.sum(p, axis=-1, keepdims=True)
            mix = dot(p.astype(BF16), kv_pad[s, window, C_ATOM:]) / total
            mixed.append(
                jnp.sum(mix.reshape(HEADS_A, Q_WIN, C_ATOM) * head_mask, axis=0)
            )
        rows = slice(s * A_DEV, (s + 1) * A_DEV)
        mix = jnp.concatenate(mixed, axis=0).astype(BF16)
        atom_enc[rows] = atom_enc[rows] + dot(mix, atom_out[...])

    slot_index = atom_token[...] - (d * TOK_DEV - TOK_DEV)
    member = jnp.where(
        slot_index == iota((2 * TOK_DEV, A_DEV), 0), 1.0, 0.0
    )
    member_low = member.astype(BF16)
    hidden = jnp.maximum(dot(atom_enc[...].astype(BF16), w_agg[...]), 0.0)
    for s in range(SAMPLES):
        mine = hidden[s * A_DEV : (s + 1) * A_DEV]
        high = mine.astype(BF16)
        low = (mine - high.astype(F32)).astype(BF16)
        sums = dot(
            jnp.concatenate([member_low, member_low], axis=1),
            jnp.concatenate([high, low], axis=0),
        )
        spill_out[s] = sums[0:TOK_DEV].astype(BF16)
        token_act[s] = sums[TOK_DEV : 2 * TOK_DEV]
    spill = pltpu.make_async_remote_copy(
        src_ref=spill_out,
        dst_ref=spill_in,
        send_sem=spill_sems.at[0],
        recv_sem=spill_sems.at[1],
        device_id=down_id,
        device_id_type=MESH,
    )
    spill.start()
    pair_bias(6, 11)
    lanes = iota((D_TOK, 2 * C_ATOM), 0)
    head_of = lax.rem(iota((D_TOK, 2 * C_ATOM), 1), C_ATOM)
    expand[...] = jnp.where(
        (lanes >= head_of * HEAD) & (lanes < head_of * HEAD + HEAD), 1.0, 0.0
    ).astype(BF16)
    diagonal = iota((TOK_DEV, TOK_DEV), 0) == iota((TOK_DEV, TOK_DEV), 1)
    counts = jnp.sum(
        jnp.where(diagonal, token_counts[...].astype(F32), 0.0), axis=1, keepdims=True
    )
    spill.wait()
    for s in range(SAMPLES):
        token_act[s] = (token_act[s] + spill_in[s].astype(F32)) / counts

    def q_copy(b, s, j):
        return pltpu.make_async_remote_copy(
            src_ref=q_all.at[b, s, c],
            dst_ref=q_all.at[b, s, c],
            send_sem=q_send.at[b, s, j],
            recv_sem=q_recv.at[b, s, c],
            device_id=(r, lax.rem(c + j, COLS)),
            device_id_type=MESH,
        )

    def q_arrival(b, s, j):
        peer = lax.rem(c + j, COLS)
        return pltpu.make_async_remote_copy(
            src_ref=q_all.at[b, s, peer],
            dst_ref=q_all.at[b, s, peer],
            send_sem=q_send.at[b, s, j],
            recv_sem=q_recv.at[b, s, peer],
            device_id=(r, peer),
            device_id_type=MESH,
        )

    def turn_copy(b, s):
        return pltpu.make_async_remote_copy(
            src_ref=q_all.at[b, s, c],
            dst_ref=kv_all.at[b, s, turn_slot],
            send_sem=turn_send.at[b, s],
            recv_sem=turn_recv.at[b, s],
            device_id=turn_to,
            device_id_type=MESH,
        )

    def turn_arrival(b, s):
        return pltpu.make_async_remote_copy(
            src_ref=q_all.at[b, s, c],
            dst_ref=kv_all.at[b, s, slot],
            send_sem=turn_send.at[b, s],
            recv_sem=turn_recv.at[b, s],
            device_id=turn_from,
            device_id_type=MESH,
        )

    def kv_copy(b, s, j):
        return pltpu.make_async_remote_copy(
            src_ref=kv_all.at[b, s, slot],
            dst_ref=kv_all.at[b, s, slot],
            send_sem=kv_send.at[b, s, j],
            recv_sem=kv_recv.at[b, s, level_r],
            device_id=(lax.rem(r + 2 * j, ROWS), c),
            device_id_type=MESH,
        )

    def kv_arrival(b, s, j):
        peer = lax.rem(r + 2 * j, ROWS)
        peer_slot = core * COLS + swap2(lax.div(peer, 2))
        return pltpu.make_async_remote_copy(
            src_ref=kv_all.at[b, s, peer_slot],
            dst_ref=kv_all.at[b, s, peer_slot],
            send_sem=kv_send.at[b, s, j],
            recv_sem=kv_recv.at[b, s, lax.div(peer, 2)],
            device_id=(peer, c),
            device_id_type=MESH,
        )

    def twin_copy(b, s, half):
        blocks = pl.ds(half * COLS, COLS)
        return pltpu.make_async_remote_copy(
            src_ref=kv_all.at[b, s, blocks],
            dst_ref=kv_all.at[b, s, blocks],
            send_sem=twin_send.at[b, s],
            recv_sem=twin_recv.at[b, s],
            device_id=twin_id,
            device_id_type=MESH,
        )

    def part_copy(b, s, j):
        peer = lax.rem(c + j, COLS)
        return pltpu.make_async_remote_copy(
            src_ref=part.at[b, s, peer],
            dst_ref=part_in.at[b, s, c],
            send_sem=part_send.at[b, s, j],
            recv_sem=part_recv.at[b, s, c],
            device_id=(r, peer),
            device_id_type=MESH,
        )

    def part_arrival(b, s, j):
        peer = lax.rem(c + j, COLS)
        return pltpu.make_async_remote_copy(
            src_ref=part.at[b, s, peer],
            dst_ref=part_in.at[b, s, peer],
            send_sem=part_send.at[b, s, j],
            recv_sem=part_recv.at[b, s, peer],
            device_id=(r, peer),
            device_id_type=MESH,
        )

    def send_normed(b, s):
        q_all[b, s, c] = layer_norm(token_act[s]).astype(BF16)
        turn_copy(b, s).start()

    def send_queries(b, s):
        each(1, COLS, lambda j: q_copy(b, s, j).start())

    def pass_on(b, s):
        turn_arrival(b, s).wait_recv()
        each(1, ROWS // 2, lambda j: kv_copy(b, s, j).start())

    def gate(b, s):
        g = dot(q_all[b, s, c], proj[b, :, 3 * D_TOK :]).astype(BF16).astype(F32)
        gates[s] = 1.0 / (1.0 + jnp.exp(-g))

    def project_queries(b, s):
        each(1, COLS, lambda j: q_arrival(b, s, j).wait_recv())
        normed = q_all[b, s].reshape(QUERIES, D_TOK)
        for n in range(0, D_TOK, 256):
            q_ref[s, :, n : n + 256] = (
                dot(normed, proj[b, :, n : n + 256]) * (LOG2E / math.sqrt(HEAD))
            ).astype(BF16)

    def share(b, s):
        each(1, ROWS // 2, lambda j: kv_arrival(b, s, j).wait_recv())
        twin_copy(b, s, core).start()

    def project_keys(b, s, half):
        normed = kv_all[b, s, pl.ds(half * COLS, COLS)].reshape(KEYS // 2, D_TOK)
        rows = pl.ds(pl.multiple_of(half * (KEYS // 2), KEYS // 2), KEYS // 2)
        for n in range(0, D_TOK, 256):
            at = D_TOK + n
            k_ref[s, n : n + 256, rows] = dot(normed, proj[b, :, at : at + 256]).T.astype(BF16)
            at = 2 * D_TOK + n
            v_ref[s, rows, n : n + 256] = dot(normed, proj[b, :, at : at + 256]).astype(BF16)

    def attention(b, s):
        project_keys(b, s, core)
        twin_copy(b, s, 1 - core).wait_recv()
        project_keys(b, s, 1 - core)
        stat[...] = jnp.zeros_like(stat)
        lane = iota((QUERIES, C_ATOM), 1)

        def group(g, _):
            base = g * (8 * HEAD)
            outs = []
            stats = stat[...]
            for hh, (tile, tiles) in enumerate(HEAD_TILES):
                window = pl.ds(base + tile * 128, tiles * 128)
                at = iota((16, tiles * 128), 1) + tile * 128
                mine = jnp.where((at >= hh * HEAD) & (at < (hh + 1) * HEAD), 1.0, 0.0)
                query = q_ref[s, :, window].reshape(QUERIES // 16, 16, tiles * 128)
                query = (query * mine.astype(BF16)[None]).reshape(QUERIES, tiles * 128)
                rows = pl.ds((b * HEADS + g * 8 + hh) * STRIDE, QUERIES)
                score = dot(query, k_ref[s, window, :]) + jnp.concatenate(
                    [bias[t, rows, :] for t in range(KEYS // 128)], axis=1
                )
                top = jnp.max(score, axis=-1, keepdims=True)
                p = jnp.exp2(score - top)
                total = jnp.sum(p, axis=-1, keepdims=True)
                outs.append(dot(p.astype(BF16), v_ref[s, :, window]))
                stats = jnp.where(lane == g * 8 + hh, top, stats)
                stats = jnp.where(lane == HEADS + g * 8 + hh, total, stats)
            stat[...] = stats
            o0, o1, o2, o3, o4, o5, o6, o7 = outs
            tiles = (
                jnp.where(lane < 48, o0, jnp.where(lane < 96, o1, o2[:, :128])),
                jnp.where(
                    lane < 16,
                    o2[:, 128:],
                    jnp.where(lane < 64, o3, jnp.where(lane < 112, o4, o5[:, :128])),
                ),
                jnp.where(lane < 32, o5[:, 128:], jnp.where(lane < 80, o6, o7)),
            )
            for t, value in enumerate(tiles):
                where = pl.ds(base + t * 128, 128)
                part[b, s, :, :, where] = value.astype(BF16).reshape(COLS, TOK_DEV, 128)
            return 0

        group(0, 0)
        group(1, 0)
        exact = stat[...]
        high = exact.astype(BF16).astype(F32)
        rest = exact - high
        mid = rest.astype(BF16).astype(F32)
        pieces = high + pltpu.roll(mid, 32, 1) + pltpu.roll(rest - mid, 64, 1)
        part[b, s, :, :, D_TOK:PART] = pieces.astype(BF16).reshape(COLS, TOK_DEV, 128)
        each(1, COLS, lambda j: part_copy(b, s, j).start())
        part_in[b, s, c] = part[b, s, c]

    def combine(b, s):
        each(1, COLS, lambda j: part_arrival(b, s, j).wait_recv())
        pieces = part_in[b, s, :, :, D_TOK:PART].astype(F32).reshape(QUERIES, 128)
        stats = pieces + pltpu.roll(pieces, 96, 1) + pltpu.roll(pieces, 64, 1)
        stats = stats.reshape(COLS, TOK_DEV, 128)
        weight = jnp.exp2(stats - jnp.max(stats, axis=0, keepdims=True))
        dens = pltpu.roll(stats.reshape(QUERIES, 128), 128 - HEADS, 1).reshape(stats.shape)
        total = jnp.sum(weight * dens, axis=0, keepdims=True)
        weight = jnp.where(iota(stats.shape, 2) < HEADS, weight / total, 0.0)
        weight = weight.reshape(QUERIES, 128)
        high = weight.astype(BF16)
        low = (weight - high.astype(F32)).astype(BF16)
        spread = dot(jnp.concatenate([high, low], axis=1), expand[...], ((1,), (1,)))
        nums = part_in[b, s, :, :, 0:D_TOK].astype(F32)
        mix = jnp.sum(nums * spread.reshape(COLS, TOK_DEV, D_TOK), axis=0)
        gated = (gates[s] * mix).astype(BF16)
        token_act[s] = token_act[s] + dot(gated, tok_out[b])

    samples = range(SAMPLES)
    for s in samples:
        send_normed(0, s)
    for s in samples:
        send_queries(0, s)
    pair_bias(11, 16)
    for b in range(BLOCKS):
        for s in samples:
            pass_on(b, s)
        proj_copies[b].wait()
        for s in samples:
            gate(b, s)
        for s in samples:
            project_queries(b, s)
        for s in samples:
            share(b, s)
        for s in samples:
            attention(b, s)
        out_copies[b].wait()
        for s in samples:
            combine(b, s)
            if b + 1 < BLOCKS:
                send_normed(b + 1, s)
                send_queries(b + 1, s)

    for s in range(SAMPLES):
        dec_out[s] = dot(token_act[s].astype(BF16), w_dec[...])
    decoded = pltpu.make_async_remote_copy(
        src_ref=dec_out,
        dst_ref=dec_in,
        send_sem=dec_sems.at[0],
        recv_sem=dec_sems.at[1],
        device_id=up_id,
        device_id_type=MESH,
    )
    decoded.start()
    for b in range(BLOCKS):
        for s in range(SAMPLES):
            each(1, COLS, lambda j: q_copy(b, s, j).wait_send())
            turn_copy(b, s).wait_send()
            each(1, ROWS // 2, lambda j: kv_copy(b, s, j).wait_send())
            twin_copy(b, s, core).wait_send()
            each(1, COLS, lambda j: part_copy(b, s, j).wait_send())

    decoded.wait()
    member3 = jnp.concatenate([member_low] * 3, axis=0)
    for s in range(SAMPLES):
        table = jnp.concatenate([dec_in[s], dec_out[s]], axis=0)
        high = table.astype(BF16)
        rest = table - high.astype(F32)
        mid = rest.astype(BF16)
        low = (rest - mid.astype(F32)).astype(BF16)
        picked = dot(member3, jnp.concatenate([high, mid, low], axis=0), ((0,), (0,)))
        atom_dec = atom_enc[s * A_DEV : (s + 1) * A_DEV] + picked
        update = dot(w_update[...], layer_norm(atom_dec).astype(BF16), ((1,), (1,)))
        level = jnp.broadcast_to(noise_level[:, s : s + 1], (1, A_DEV))
        noisy = atom_pos[:, s] + level * noise[:, s]
        square = level * level + 1.0
        out[:, s] = noisy / square + level / jnp.sqrt(square) * update


def body(
    atom_pos,
    noise,
    noise_level,
    atom_single,
    w_pos,
    atom_bias,
    atom_qkv,
    atom_out,
    w_agg,
    atom_token,
    token_counts,
    pair,
    w_pairbias,
    tok_proj,
    tok_out,
    w_dec,
    w_update,
):
    vmem = pl.BlockSpec(memory_space=pltpu.VMEM)
    hbm = pl.BlockSpec(memory_space=pl.ANY)
    dma = pltpu.SemaphoreType.DMA
    denoised = pl.pallas_call(
        kernel,
        out_shape=jax.ShapeDtypeStruct((3, SAMPLES, A_DEV), F32),
        in_specs=[hbm] * 17,
        out_specs=vmem,
        scratch_shapes=[
            pltpu.VMEM((1, SAMPLES), F32),
            pltpu.VMEM((3, SAMPLES, A_DEV), F32),
            pltpu.VMEM((3, SAMPLES, A_DEV), F32),
            pltpu.VMEM((A_DEV, C_ATOM), BF16),
            pltpu.VMEM((3, C_ATOM), F32),
            pltpu.VMEM((HEADS_A, A_DEV, K_WIN), BF16),
            pltpu.VMEM((C_ATOM, 3 * C_ATOM), BF16),
            pltpu.VMEM((C_ATOM, C_ATOM), BF16),
            pltpu.VMEM((C_ATOM, D_TOK), BF16),
            pltpu.VMEM((1, A_DEV), jnp.int32),
            pltpu.VMEM((1, TOK_DEV), jnp.int32),
            pltpu.VMEM((2 * HEADS, C_ATOM), BF16),
            pltpu.VMEM((D_TOK, C_ATOM), BF16),
            pltpu.VMEM((3, C_ATOM), BF16),
            pltpu.VMEM((QUERIES, KEYS, C_ATOM), BF16),
            pltpu.VMEM((BLOCKS, D_TOK, 4 * D_TOK), BF16),
            pltpu.VMEM((BLOCKS, D_TOK, D_TOK), BF16),
            pltpu.VMEM((KEYS // 128, 2 * HEADS * STRIDE, 128), F32),
            pltpu.VMEM((8 * C_ATOM, KEYS), BF16),
            pltpu.VMEM((KEYS, KEYS), BF16),
            pltpu.VMEM((D_TOK, 2 * C_ATOM), BF16),
            pltpu.VMEM((SAMPLES * A_DEV, C_ATOM), F32),
            pltpu.VMEM((SAMPLES, A_DEV, C_ATOM), BF16),
            pltpu.VMEM((SAMPLES, A_DEV, 2 * C_ATOM), BF16),
            pltpu.VMEM((2, SAMPLES, MARGIN, 2 * C_ATOM), BF16),
            pltpu.VMEM((SAMPLES, A_DEV + 2 * MARGIN, 2 * C_ATOM), BF16),
            pltpu.VMEM((SAMPLES, TOK_DEV, D_TOK), BF16),
            pltpu.VMEM((SAMPLES, TOK_DEV, D_TOK), BF16),
            pltpu.VMEM((SAMPLES, TOK_DEV, D_TOK), F32),
            pltpu.VMEM((SAMPLES, TOK_DEV, D_TOK), F32),
            pltpu.VMEM((BLOCKS, SAMPLES, COLS, TOK_DEV, D_TOK), BF16),
            pltpu.VMEM((BLOCKS, SAMPLES, ROWS, TOK_DEV, D_TOK), BF16),
            pltpu.VMEM((SAMPLES, QUERIES, D_TOK), BF16),
            pltpu.VMEM((SAMPLES, D_TOK, KEYS), BF16),
            pltpu.VMEM((SAMPLES, KEYS, D_TOK), BF16),
            pltpu.VMEM((QUERIES, 128), F32),
            pltpu.VMEM((BLOCKS, SAMPLES, COLS, TOK_DEV, PART), BF16),
            pltpu.VMEM((BLOCKS, SAMPLES, COLS, TOK_DEV, PART), BF16),
            pltpu.VMEM((SAMPLES, TOK_DEV, C_ATOM), F32),
            pltpu.VMEM((SAMPLES, TOK_DEV, C_ATOM), F32),
            dma((14,)),
            dma((4,)),
            dma((4,)),
            dma((2,)),
            dma((2,)),
            dma((2,)),
            dma((2,)),
            dma((BLOCKS, SAMPLES)),
            dma((BLOCKS, SAMPLES)),
            dma((BLOCKS, SAMPLES, COLS)),
            dma((BLOCKS, SAMPLES, COLS)),
            dma((BLOCKS, SAMPLES, ROWS // 2)),
            dma((BLOCKS, SAMPLES, ROWS // 2)),
            dma((BLOCKS, SAMPLES)),
            dma((BLOCKS, SAMPLES)),
            dma((BLOCKS, SAMPLES, COLS)),
            dma((BLOCKS, SAMPLES, COLS)),
        ],
        compiler_params=pltpu.CompilerParams(
            collective_id=0, has_side_effects=True, vmem_limit_bytes=56 * 1024 * 1024
        ),
    )(
        noise_level.reshape(1, SAMPLES),
        atom_pos.transpose(1, 0, 2),
        noise.transpose(1, 0, 2),
        atom_single,
        w_pos,
        atom_bias,
        atom_qkv,
        atom_out,
        w_agg,
        atom_token.reshape(1, A_DEV),
        token_counts.reshape(1, TOK_DEV),
        pair,
        w_pairbias.T,
        tok_proj,
        tok_out,
        w_dec,
        w_update.T,
    )
    return denoised.transpose(1, 0, 2)


def solution(mesh):
    return jax.shard_map(
        body,
        mesh=mesh,
        in_specs=(
            P(None, None, ("row", "col")),
            P(None, None, ("row", "col")),
            P(),
            P(("row", "col"), None),
            P(),
            P(None, ("row", "col"), None),
            P(),
            P(),
            P(),
            P(("row", "col")),
            P(("row", "col")),
            P("row", "col", None),
            P(),
            P(),
            P(),
            P(),
            P(),
        ),
        out_specs=P(None, None, ("row", "col")),
        check_vma=False,
    )
```

```python
import math

import jax
import jax.numpy as jnp
from jax import lax
from jax.experimental import pallas as pl
from jax.experimental.pallas import tpu as pltpu
from jax.sharding import PartitionSpec as P

HEADS = 16
HEAD = 48
D_TOK = 768
HEADS_A = 4
HEAD_A = 32
C_ATOM = 128
Q_WIN = 32
K_WIN = 128
MARGIN = 48
BLOCKS = 2
SAMPLES = 2
TOK_DEV = 16
A_DEV = 128
ROWS = 16
COLS = 8
DEVICES = ROWS * COLS
QUERIES = COLS * TOK_DEV
KEYS = ROWS * TOK_DEV
PART = D_TOK + 128
STRIDE = QUERIES + 8
LN_EPSILON = 1e-05
LOG2E = math.log2(math.e)
MESH = pl.DeviceIdType.MESH
F32 = jnp.float32
BF16 = jnp.bfloat16

HEAD_TILES = ((0, 1), (0, 1), (0, 2), (1, 1), (1, 1), (1, 2), (2, 1), (2, 1))


def dot(a, b, dims=((1,), (0,)), precision=None):
    return lax.dot_general(
        a, b, (dims, ((), ())), precision=precision, preferred_element_type=F32
    )


def iota(shape, dim):
    return lax.broadcasted_iota(jnp.int32, shape, dim)


def layer_norm(v):
    mean = jnp.mean(v, axis=-1, keepdims=True)
    centred = v - mean
    var = jnp.mean(centred * centred, axis=-1, keepdims=True)
    return centred * lax.rsqrt(var + LN_EPSILON)


def swap2(i):
    return i + 2 - 4 * lax.rem(lax.div(i, 2), 2)


def kernel(
    noise_level_hbm,
    atom_pos_hbm,
    noise_hbm,
    atom_single_hbm,
    w_pos_hbm,
    atom_bias_hbm,
    atom_qkv_hbm,
    atom_out_hbm,
    w_agg_hbm,
    atom_token_hbm,
    token_counts_hbm,
    pair_hbm,
    w_pairbias_hbm,
    tok_proj_hbm,
    tok_out_hbm,
    w_dec_hbm,
    w_update_hbm,
    out,
    noise_level,
    atom_pos,
    noise,
    atom_single,
    w_pos,
    atom_bias,
    atom_qkv,
    atom_out,
    w_agg,
    atom_token,
    token_counts,
    w_pairbias,
    w_dec,
    w_update,
    pair,
    proj,
    tok_out,
    bias,
    w_spread,
    centre,
    expand,
    atom_enc,
    queries_a,
    kv_own,
    halo,
    kv_pad,
    spill_out,
    spill_in,
    token_act,
    gates,
    q_all,
    kv_all,
    q_ref,
    k_ref,
    v_ref,
    stat,
    part,
    part_in,
    dec_out,
    dec_in,
    input_sem,
    pair_sem,
    weight_sem,
    halo_send,
    halo_recv,
    spill_sems,
    dec_sems,
    turn_send,
    turn_recv,
    q_send,
    q_recv,
    kv_send,
    kv_recv,
    twin_send,
    twin_recv,
    part_send,
    part_recv,
):
    r = lax.axis_index("row")
    c = lax.axis_index("col")
    d = r * COLS + c
    up = lax.rem(d + 1, DEVICES)
    down = lax.rem(d + DEVICES - 1, DEVICES)
    up_id = (lax.div(up, COLS), lax.rem(up, COLS))
    down_id = (lax.div(down, COLS), lax.rem(down, COLS))
    core = lax.rem(r, 2)
    level_r = lax.div(r, 2)
    twin_id = (r + 1 - 2 * core, c)
    turn_to = (2 * swap2(c) + core, level_r)
    turn_from = (2 * c + core, swap2(level_r))
    slot = core * COLS + swap2(level_r)
    turn_slot = core * COLS + c

    barrier = pltpu.get_barrier_semaphore()

    def greet(device):
        pl.semaphore_signal(barrier, inc=1, device_id=device, device_id_type=MESH)

    def each(first, last, act):
        def step(j, _):
            act(j)
            return 0

        lax.fori_loop(first, last, step, 0)

    greet(turn_from)
    greet(up_id)
    greet(down_id)
    each(1, COLS, lambda j: greet((r, lax.rem(c + j, COLS))))
    each(1, ROWS // 2, lambda j: greet((lax.rem(r + 2 * j, ROWS), c)))
    greet(twin_id)

    small = [
        (noise_level_hbm, noise_level),
        (atom_pos_hbm, atom_pos),
        (noise_hbm, noise),
        (atom_single_hbm, atom_single),
        (w_pos_hbm, w_pos),
        (atom_qkv_hbm, atom_qkv),
        (w_pairbias_hbm, w_pairbias),
        (atom_bias_hbm, atom_bias),
        (atom_out_hbm, atom_out),
        (w_agg_hbm, w_agg),
        (atom_token_hbm, atom_token),
        (token_counts_hbm, token_counts),
        (w_dec_hbm, w_dec),
        (w_update_hbm, w_update),
    ]
    small_copies = [
        pltpu.make_async_copy(a, b, input_sem.at[i]) for i, (a, b) in enumerate(small)
    ]
    for copy in small_copies:
        copy.start()

    def pair_copy(i):
        rows = pl.ds(i * 32, 32)
        return pltpu.make_async_copy(pair_hbm.at[rows], pair.at[rows], pair_sem.at[i])

    proj_copies = [
        pltpu.make_async_copy(tok_proj_hbm.at[b], proj.at[b], weight_sem.at[b]) for b in range(2)
    ]
    out_copies = [
        pltpu.make_async_copy(tok_out_hbm.at[b], tok_out.at[b], weight_sem.at[2 + b])
        for b in range(2)
    ]
    for i in range(4):
        pair_copy(i).start()
    for b in range(2):
        proj_copies[b].start()
        out_copies[b].start()
    for copy in small_copies[:7]:
        copy.wait()

    row_i, col_i = iota((KEYS, KEYS), 0), iota((KEYS, KEYS), 1)
    same = row_i // C_ATOM == col_i // C_ATOM
    centre[...] = (
        jnp.where(row_i == col_i, 1.0, 0.0) - jnp.where(same, 1.0 / C_ATOM, 0.0)
    ).astype(BF16)
    heads_wide = iota((2 * HEADS, KEYS), 1) // 8 == iota((2 * HEADS, KEYS), 0)
    wide = dot(w_pairbias[...], jnp.where(heads_wide, 1.0, 0.0).astype(BF16), ((0,), (0,)))
    query_of = lax.rem(iota((C_ATOM, KEYS), 1), 8)
    for q in range(8):
        w_spread[q * C_ATOM : (q + 1) * C_ATOM, :] = jnp.where(query_of == q, wide, 0.0).astype(
            BF16
        )

    def pair_bias(first, last):
        def step(i, _):
            q0 = pl.multiple_of(i * 8, 8)
            centred, squares = [], []
            for p in range(4):
                two = jnp.concatenate([pair[q0 + 2 * p], pair[q0 + 2 * p + 1]], axis=1)
                part_centred = dot(two, centre[...])
                centred.append(part_centred.astype(BF16))
                squares.append(part_centred * part_centred)
            y = dot(jnp.concatenate(centred, axis=1), w_spread[...])
            query = lax.rem(iota((KEYS, C_ATOM), 1), 8)
            total = jnp.zeros((KEYS, C_ATOM), F32)
            for q in range(8):
                half = slice((q % 2) * C_ATOM, (q % 2 + 1) * C_ATOM)
                mine = jnp.sum(squares[q // 2][:, half], axis=1, keepdims=True)
                total = jnp.where(query == q, mine, total)
            scale = lax.rsqrt(total * (1.0 / C_ATOM) + LN_EPSILON) * LOG2E
            turned = (y * jnp.concatenate([scale, scale], axis=1)).T
            for t in range(KEYS // 128):
                for h in range(2 * HEADS):
                    bias[t, pl.ds(pl.multiple_of(h * STRIDE + q0, 8), 8), :] = turned[
                        h * 8 : (h + 1) * 8, t * 128 : (t + 1) * 128
                    ]
            return 0

        lax.fori_loop(first, last, step, 0)

    acts = []
    for s in range(SAMPLES):
        level = jnp.broadcast_to(noise_level[:, s : s + 1], (1, A_DEV))
        noisy = atom_pos[:, s] + level * noise[:, s]
        scaled = noisy / jnp.sqrt(level * level + 1.0)
        acts.append(
            atom_single[...].astype(F32)
            + dot(scaled, w_pos[...], ((0,), (0,)), lax.Precision.HIGHEST)
        )
    act = jnp.concatenate(acts, axis=0)
    atom_enc[...] = act
    projected = dot(layer_norm(act).astype(BF16), atom_qkv[...]).astype(BF16)
    for s in range(SAMPLES):
        rows = slice(s * A_DEV, (s + 1) * A_DEV)
        queries_a[s] = projected[rows, 0:C_ATOM]
        kv_own[s] = projected[rows, C_ATOM:]
    pl.semaphore_wait(barrier, 1 + 2 + (COLS - 1) + (ROWS // 2 - 1) + 1)

    def halo_copies():
        return (
            pltpu.make_async_remote_copy(
                src_ref=kv_own.at[:, pl.ds(A_DEV - MARGIN, MARGIN)],
                dst_ref=halo.at[0],
                send_sem=halo_send.at[0],
                recv_sem=halo_recv.at[0],
                device_id=up_id,
                device_id_type=MESH,
            ),
            pltpu.make_async_remote_copy(
                src_ref=kv_own.at[:, pl.ds(0, MARGIN)],
                dst_ref=halo.at[1],
                send_sem=halo_send.at[1],
                recv_sem=halo_recv.at[1],
                device_id=down_id,
                device_id_type=MESH,
            ),
        )

    to_up, to_down = halo_copies()
    to_up.start()
    to_down.start()
    for i in range(4):
        pair_copy(i).wait()
    pair_bias(0, 6)
    for copy in small_copies[7:]:
        copy.wait()
    to_up.wait()
    to_down.wait()
    for s in range(SAMPLES):
        kv_pad[s, 0:MARGIN] = halo[0, s]
        kv_pad[s, MARGIN : MARGIN + A_DEV] = kv_own[s]
        kv_pad[s, MARGIN + A_DEV : A_DEV + 2 * MARGIN] = halo[1, s]

    lane_head = iota((HEADS_A, Q_WIN, C_ATOM), 2) // HEAD_A == iota((HEADS_A, Q_WIN, C_ATOM), 0)
    head_mask = jnp.where(lane_head, 1.0, 0.0)
    head_mask_low = head_mask.astype(BF16)
    slots = iota((1, K_WIN), 1)
    windows = [(s, w) for s in range(SAMPLES) for w in range(A_DEV // Q_WIN)]
    scores = []
    for s, w in windows:
        rows = slice(w * Q_WIN, (w + 1) * Q_WIN)
        keys = kv_pad[s, w * Q_WIN : w * Q_WIN + K_WIN, 0:C_ATOM]
        query = (queries_a[s, rows][None] * head_mask_low).reshape(HEADS_A * Q_WIN, C_ATOM)
        scores.append(dot(query, keys, ((1,), (1,))))
    weights = []
    for (s, w), score in zip(windows, scores):
        rows = slice(w * Q_WIN, (w + 1) * Q_WIN)
        score = score * (1 / math.sqrt(HEAD_A))
        score = score + atom_bias[:, rows, :].astype(F32).reshape(HEADS_A * Q_WIN, K_WIN)
        index = d * A_DEV + w * Q_WIN - MARGIN + slots
        inside = (index >= 0) & (index < DEVICES * A_DEV)
        score = jnp.where(inside, score, -1e30)
        p = jnp.exp(score - jnp.max(score, axis=-1, keepdims=True))
        weights.append((p.astype(BF16), jnp.sum(p, axis=-1, keepdims=True)))
    mixed = []
    for (s, w), (p, total) in zip(windows, weights):
        mix = dot(p, kv_pad[s, w * Q_WIN : w * Q_WIN + K_WIN, C_ATOM:]) / total
        mixed.append(jnp.sum(mix.reshape(HEADS_A, Q_WIN, C_ATOM) * head_mask, axis=0))
    atom_enc[...] = atom_enc[...] + dot(
        jnp.concatenate(mixed, axis=0).astype(BF16), atom_out[...]
    )

    slot_index = atom_token[...] - (d * TOK_DEV - TOK_DEV)
    member = jnp.where(
        slot_index == iota((2 * TOK_DEV, A_DEV), 0), 1.0, 0.0
    )
    member_low = member.astype(BF16)
    hidden = jnp.maximum(dot(atom_enc[...].astype(BF16), w_agg[...]), 0.0)
    for s in range(SAMPLES):
        mine = hidden[s * A_DEV : (s + 1) * A_DEV]
        high = mine.astype(BF16)
        low = (mine - high.astype(F32)).astype(BF16)
        sums = dot(
            jnp.concatenate([member_low, member_low], axis=1),
            jnp.concatenate([high, low], axis=0),
        )
        spill_out[s] = sums[0:TOK_DEV].astype(BF16)
        token_act[s] = sums[TOK_DEV : 2 * TOK_DEV]
    spill = pltpu.make_async_remote_copy(
        src_ref=spill_out,
        dst_ref=spill_in,
        send_sem=spill_sems.at[0],
        recv_sem=spill_sems.at[1],
        device_id=down_id,
        device_id_type=MESH,
    )
    spill.start()
    pair_bias(6, 11)
    lanes = iota((D_TOK, 2 * C_ATOM), 0)
    head_of = lax.rem(iota((D_TOK, 2 * C_ATOM), 1), C_ATOM)
    expand[...] = jnp.where(
        (lanes >= head_of * HEAD) & (lanes < head_of * HEAD + HEAD), 1.0, 0.0
    ).astype(BF16)
    diagonal = iota((TOK_DEV, TOK_DEV), 0) == iota((TOK_DEV, TOK_DEV), 1)
    counts = jnp.sum(
        jnp.where(diagonal, token_counts[...].astype(F32), 0.0), axis=1, keepdims=True
    )
    spill.wait()
    for s in range(SAMPLES):
        token_act[s] = (token_act[s] + spill_in[s].astype(F32)) / counts

    def q_copy(b, s, j):
        return pltpu.make_async_remote_copy(
            src_ref=q_all.at[b, s, c],
            dst_ref=q_all.at[b, s, c],
            send_sem=q_send.at[b, s, j],
            recv_sem=q_recv.at[b, s, c],
            device_id=(r, lax.rem(c + j, COLS)),
            device_id_type=MESH,
        )

    def q_arrival(b, s, j):
        peer = lax.rem(c + j, COLS)
        return pltpu.make_async_remote_copy(
            src_ref=q_all.at[b, s, peer],
            dst_ref=q_all.at[b, s, peer],
            send_sem=q_send.at[b, s, j],
            recv_sem=q_recv.at[b, s, peer],
            device_id=(r, peer),
            device_id_type=MESH,
        )

    def turn_copy(b, s):
        return pltpu.make_async_remote_copy(
            src_ref=q_all.at[b, s, c],
            dst_ref=kv_all.at[b, s, turn_slot],
            send_sem=turn_send.at[b, s],
            recv_sem=turn_recv.at[b, s],
            device_id=turn_to,
            device_id_type=MESH,
        )

    def turn_arrival(b, s):
        return pltpu.make_async_remote_copy(
            src_ref=q_all.at[b, s, c],
            dst_ref=kv_all.at[b, s, slot],
            send_sem=turn_send.at[b, s],
            recv_sem=turn_recv.at[b, s],
            device_id=turn_from,
            device_id_type=MESH,
        )

    def kv_copy(b, s, j):
        return pltpu.make_async_remote_copy(
            src_ref=kv_all.at[b, s, slot],
            dst_ref=kv_all.at[b, s, slot],
            send_sem=kv_send.at[b, s, j],
            recv_sem=kv_recv.at[b, s, level_r],
            device_id=(lax.rem(r + 2 * j, ROWS), c),
            device_id_type=MESH,
        )

    def kv_arrival(b, s, j):
        peer = lax.rem(r + 2 * j, ROWS)
        peer_slot = core * COLS + swap2(lax.div(peer, 2))
        return pltpu.make_async_remote_copy(
            src_ref=kv_all.at[b, s, peer_slot],
            dst_ref=kv_all.at[b, s, peer_slot],
            send_sem=kv_send.at[b, s, j],
            recv_sem=kv_recv.at[b, s, lax.div(peer, 2)],
            device_id=(peer, c),
            device_id_type=MESH,
        )

    def twin_copy(b, s, half):
        blocks = pl.ds(half * COLS, COLS)
        return pltpu.make_async_remote_copy(
            src_ref=kv_all.at[b, s, blocks],
            dst_ref=kv_all.at[b, s, blocks],
            send_sem=twin_send.at[b, s],
            recv_sem=twin_recv.at[b, s],
            device_id=twin_id,
            device_id_type=MESH,
        )

    def part_copy(b, s, j):
        peer = lax.rem(c + j, COLS)
        return pltpu.make_async_remote_copy(
            src_ref=part.at[b, s, peer],
            dst_ref=part_in.at[b, s, c],
            send_sem=part_send.at[b, s, j],
            recv_sem=part_recv.at[b, s, c],
            device_id=(r, peer),
            device_id_type=MESH,
        )

    def part_arrival(b, s, j):
        peer = lax.rem(c + j, COLS)
        return pltpu.make_async_remote_copy(
            src_ref=part.at[b, s, peer],
            dst_ref=part_in.at[b, s, peer],
            send_sem=part_send.at[b, s, j],
            recv_sem=part_recv.at[b, s, peer],
            device_id=(r, peer),
            device_id_type=MESH,
        )

    def send_normed(b, s):
        q_all[b, s, c] = layer_norm(token_act[s]).astype(BF16)
        turn_copy(b, s).start()

    def send_queries(b, s):
        each(1, COLS, lambda j: q_copy(b, s, j).start())

    def pass_on(b, s):
        turn_arrival(b, s).wait_recv()
        each(1, ROWS // 2, lambda j: kv_copy(b, s, j).start())

    def gate(b, s):
        g = dot(q_all[b, s, c], proj[b, :, 3 * D_TOK :]).astype(BF16).astype(F32)
        gates[s] = 1.0 / (1.0 + jnp.exp(-g))

    def project_queries(b, s):
        each(1, COLS, lambda j: q_arrival(b, s, j).wait_recv())
        normed = q_all[b, s].reshape(QUERIES, D_TOK)
        for n in range(0, D_TOK, 256):
            q_ref[s, :, n : n + 256] = (
                dot(normed, proj[b, :, n : n + 256]) * (LOG2E / math.sqrt(HEAD))
            ).astype(BF16)

    def share(b, s):
        each(1, ROWS // 2, lambda j: kv_arrival(b, s, j).wait_recv())
        twin_copy(b, s, core).start()

    def project_keys(b, s, half):
        normed = kv_all[b, s, pl.ds(half * COLS, COLS)].reshape(KEYS // 2, D_TOK)
        rows = pl.ds(pl.multiple_of(half * (KEYS // 2), KEYS // 2), KEYS // 2)
        for n in range(0, D_TOK, 256):
            at = D_TOK + n
            k_ref[s, n : n + 256, rows] = dot(normed, proj[b, :, at : at + 256]).T.astype(BF16)
            at = 2 * D_TOK + n
            v_ref[s, rows, n : n + 256] = dot(normed, proj[b, :, at : at + 256]).astype(BF16)

    def attention(b, s):
        project_keys(b, s, core)
        twin_copy(b, s, 1 - core).wait_recv()
        project_keys(b, s, 1 - core)
        stat[...] = jnp.zeros_like(stat)
        lane = iota((QUERIES, C_ATOM), 1)

        def group(g, _):
            base = g * (8 * HEAD)
            outs = []
            stats = stat[...]
            for hh, (tile, tiles) in enumerate(HEAD_TILES):
                window = pl.ds(base + tile * 128, tiles * 128)
                at = iota((16, tiles * 128), 1) + tile * 128
                mine = jnp.where((at >= hh * HEAD) & (at < (hh + 1) * HEAD), 1.0, 0.0)
                query = q_ref[s, :, window].reshape(QUERIES // 16, 16, tiles * 128)
                query = (query * mine.astype(BF16)[None]).reshape(QUERIES, tiles * 128)
                rows = pl.ds((b * HEADS + g * 8 + hh) * STRIDE, QUERIES)
                score = dot(query, k_ref[s, window, :]) + jnp.concatenate(
                    [bias[t, rows, :] for t in range(KEYS // 128)], axis=1
                )
                top = jnp.max(score, axis=-1, keepdims=True)
                p = jnp.exp2(score - top)
                total = jnp.sum(p, axis=-1, keepdims=True)
                outs.append(dot(p.astype(BF16), v_ref[s, :, window]))
                stats = jnp.where(lane == g * 8 + hh, top, stats)
                stats = jnp.where(lane == HEADS + g * 8 + hh, total, stats)
            stat[...] = stats
            o0, o1, o2, o3, o4, o5, o6, o7 = outs
            tiles = (
                jnp.where(lane < 48, o0, jnp.where(lane < 96, o1, o2[:, :128])),
                jnp.where(
                    lane < 16,
                    o2[:, 128:],
                    jnp.where(lane < 64, o3, jnp.where(lane < 112, o4, o5[:, :128])),
                ),
                jnp.where(lane < 32, o5[:, 128:], jnp.where(lane < 80, o6, o7)),
            )
            for t, value in enumerate(tiles):
                where = pl.ds(base + t * 128, 128)
                part[b, s, :, :, where] = value.astype(BF16).reshape(COLS, TOK_DEV, 128)
            return 0

        group(0, 0)
        group(1, 0)
        exact = stat[...]
        high = exact.astype(BF16).astype(F32)
        rest = exact - high
        mid = rest.astype(BF16).astype(F32)
        pieces = high + pltpu.roll(mid, 32, 1) + pltpu.roll(rest - mid, 64, 1)
        part[b, s, :, :, D_TOK:PART] = pieces.astype(BF16).reshape(COLS, TOK_DEV, 128)
        each(1, COLS, lambda j: part_copy(b, s, j).start())
        part_in[b, s, c] = part[b, s, c]

    def combine(b, s):
        each(1, COLS, lambda j: part_arrival(b, s, j).wait_recv())
        pieces = part_in[b, s, :, :, D_TOK:PART].astype(F32).reshape(QUERIES, 128)
        stats = pieces + pltpu.roll(pieces, 96, 1) + pltpu.roll(pieces, 64, 1)
        stats = stats.reshape(COLS, TOK_DEV, 128)
        weight = jnp.exp2(stats - jnp.max(stats, axis=0, keepdims=True))
        dens = pltpu.roll(stats.reshape(QUERIES, 128), 128 - HEADS, 1).reshape(stats.shape)
        total = jnp.sum(weight * dens, axis=0, keepdims=True)
        weight = jnp.where(iota(stats.shape, 2) < HEADS, weight / total, 0.0)
        weight = weight.reshape(QUERIES, 128)
        high = weight.astype(BF16)
        low = (weight - high.astype(F32)).astype(BF16)
        spread = dot(jnp.concatenate([high, low], axis=1), expand[...], ((1,), (1,)))
        nums = part_in[b, s, :, :, 0:D_TOK].astype(F32)
        mix = jnp.sum(nums * spread.reshape(COLS, TOK_DEV, D_TOK), axis=0)
        gated = (gates[s] * mix).astype(BF16)
        token_act[s] = token_act[s] + dot(gated, tok_out[b])

    samples = range(SAMPLES)
    for s in samples:
        send_normed(0, s)
    for s in samples:
        send_queries(0, s)
    pair_bias(11, 16)
    for b in range(BLOCKS):
        for s in samples:
            pass_on(b, s)
        proj_copies[b].wait()
        for s in samples:
            gate(b, s)
        for s in samples:
            project_queries(b, s)
        for s in samples:
            share(b, s)
        for s in samples:
            attention(b, s)
        out_copies[b].wait()
        for s in samples:
            combine(b, s)
            if b + 1 < BLOCKS:
                send_normed(b + 1, s)
                send_queries(b + 1, s)

    for s in range(SAMPLES):
        dec_out[s] = dot(token_act[s].astype(BF16), w_dec[...])
    decoded = pltpu.make_async_remote_copy(
        src_ref=dec_out,
        dst_ref=dec_in,
        send_sem=dec_sems.at[0],
        recv_sem=dec_sems.at[1],
        device_id=up_id,
        device_id_type=MESH,
    )
    decoded.start()
    for b in range(BLOCKS):
        for s in range(SAMPLES):
            each(1, COLS, lambda j: q_copy(b, s, j).wait_send())
            turn_copy(b, s).wait_send()
            each(1, ROWS // 2, lambda j: kv_copy(b, s, j).wait_send())
            twin_copy(b, s, core).wait_send()
            each(1, COLS, lambda j: part_copy(b, s, j).wait_send())

    decoded.wait()
    member3 = jnp.concatenate([member_low] * 3, axis=0)
    for s in range(SAMPLES):
        table = jnp.concatenate([dec_in[s], dec_out[s]], axis=0)
        high = table.astype(BF16)
        rest = table - high.astype(F32)
        mid = rest.astype(BF16)
        low = (rest - mid.astype(F32)).astype(BF16)
        picked = dot(member3, jnp.concatenate([high, mid, low], axis=0), ((0,), (0,)))
        atom_dec = atom_enc[s * A_DEV : (s + 1) * A_DEV] + picked
        update = dot(w_update[...], layer_norm(atom_dec).astype(BF16), ((1,), (1,)))
        level = jnp.broadcast_to(noise_level[:, s : s + 1], (1, A_DEV))
        noisy = atom_pos[:, s] + level * noise[:, s]
        square = level * level + 1.0
        out[:, s] = noisy / square + level / jnp.sqrt(square) * update


def body(
    atom_pos,
    noise,
    noise_level,
    atom_single,
    w_pos,
    atom_bias,
    atom_qkv,
    atom_out,
    w_agg,
    atom_token,
    token_counts,
    pair,
    w_pairbias,
    tok_proj,
    tok_out,
    w_dec,
    w_update,
):
    vmem = pl.BlockSpec(memory_space=pltpu.VMEM)
    hbm = pl.BlockSpec(memory_space=pl.ANY)
    dma = pltpu.SemaphoreType.DMA
    denoised = pl.pallas_call(
        kernel,
        out_shape=jax.ShapeDtypeStruct((3, SAMPLES, A_DEV), F32),
        in_specs=[hbm] * 17,
        out_specs=vmem,
        scratch_shapes=[
            pltpu.VMEM((1, SAMPLES), F32),
            pltpu.VMEM((3, SAMPLES, A_DEV), F32),
            pltpu.VMEM((3, SAMPLES, A_DEV), F32),
            pltpu.VMEM((A_DEV, C_ATOM), BF16),
            pltpu.VMEM((3, C_ATOM), F32),
            pltpu.VMEM((HEADS_A, A_DEV, K_WIN), BF16),
            pltpu.VMEM((C_ATOM, 3 * C_ATOM), BF16),
            pltpu.VMEM((C_ATOM, C_ATOM), BF16),
            pltpu.VMEM((C_ATOM, D_TOK), BF16),
            pltpu.VMEM((1, A_DEV), jnp.int32),
            pltpu.VMEM((1, TOK_DEV), jnp.int32),
            pltpu.VMEM((2 * HEADS, C_ATOM), BF16),
            pltpu.VMEM((D_TOK, C_ATOM), BF16),
            pltpu.VMEM((3, C_ATOM), BF16),
            pltpu.VMEM((QUERIES, KEYS, C_ATOM), BF16),
            pltpu.VMEM((BLOCKS, D_TOK, 4 * D_TOK), BF16),
            pltpu.VMEM((BLOCKS, D_TOK, D_TOK), BF16),
            pltpu.VMEM((KEYS // 128, 2 * HEADS * STRIDE, 128), F32),
            pltpu.VMEM((8 * C_ATOM, KEYS), BF16),
            pltpu.VMEM((KEYS, KEYS), BF16),
            pltpu.VMEM((D_TOK, 2 * C_ATOM), BF16),
            pltpu.VMEM((SAMPLES * A_DEV, C_ATOM), F32),
            pltpu.VMEM((SAMPLES, A_DEV, C_ATOM), BF16),
            pltpu.VMEM((SAMPLES, A_DEV, 2 * C_ATOM), BF16),
            pltpu.VMEM((2, SAMPLES, MARGIN, 2 * C_ATOM), BF16),
            pltpu.VMEM((SAMPLES, A_DEV + 2 * MARGIN, 2 * C_ATOM), BF16),
            pltpu.VMEM((SAMPLES, TOK_DEV, D_TOK), BF16),
            pltpu.VMEM((SAMPLES, TOK_DEV, D_TOK), BF16),
            pltpu.VMEM((SAMPLES, TOK_DEV, D_TOK), F32),
            pltpu.VMEM((SAMPLES, TOK_DEV, D_TOK), F32),
            pltpu.VMEM((BLOCKS, SAMPLES, COLS, TOK_DEV, D_TOK), BF16),
            pltpu.VMEM((BLOCKS, SAMPLES, ROWS, TOK_DEV, D_TOK), BF16),
            pltpu.VMEM((SAMPLES, QUERIES, D_TOK), BF16),
            pltpu.VMEM((SAMPLES, D_TOK, KEYS), BF16),
            pltpu.VMEM((SAMPLES, KEYS, D_TOK), BF16),
            pltpu.VMEM((QUERIES, 128), F32),
            pltpu.VMEM((BLOCKS, SAMPLES, COLS, TOK_DEV, PART), BF16),
            pltpu.VMEM((BLOCKS, SAMPLES, COLS, TOK_DEV, PART), BF16),
            pltpu.VMEM((SAMPLES, TOK_DEV, C_ATOM), F32),
            pltpu.VMEM((SAMPLES, TOK_DEV, C_ATOM), F32),
            dma((14,)),
            dma((4,)),
            dma((4,)),
            dma((2,)),
            dma((2,)),
            dma((2,)),
            dma((2,)),
            dma((BLOCKS, SAMPLES)),
            dma((BLOCKS, SAMPLES)),
            dma((BLOCKS, SAMPLES, COLS)),
            dma((BLOCKS, SAMPLES, COLS)),
            dma((BLOCKS, SAMPLES, ROWS // 2)),
            dma((BLOCKS, SAMPLES, ROWS // 2)),
            dma((BLOCKS, SAMPLES)),
            dma((BLOCKS, SAMPLES)),
            dma((BLOCKS, SAMPLES, COLS)),
            dma((BLOCKS, SAMPLES, COLS)),
        ],
        compiler_params=pltpu.CompilerParams(
            collective_id=0, has_side_effects=True, vmem_limit_bytes=56 * 1024 * 1024
        ),
    )(
        noise_level.reshape(1, SAMPLES),
        atom_pos.transpose(1, 0, 2),
        noise.transpose(1, 0, 2),
        atom_single,
        w_pos,
        atom_bias,
        atom_qkv,
        atom_out,
        w_agg,
        atom_token.reshape(1, A_DEV),
        token_counts.reshape(1, TOK_DEV),
        pair,
        w_pairbias.T,
        tok_proj,
        tok_out,
        w_dec,
        w_update.T,
    )
    return denoised.transpose(1, 0, 2)


def solution(mesh):
    return jax.shard_map(
        body,
        mesh=mesh,
        in_specs=(
            P(None, None, ("row", "col")),
            P(None, None, ("row", "col")),
            P(),
            P(("row", "col"), None),
            P(),
            P(None, ("row", "col"), None),
            P(),
            P(),
            P(),
            P(("row", "col")),
            P(("row", "col")),
            P("row", "col", None),
            P(),
            P(),
            P(),
            P(),
            P(),
        ),
        out_specs=P(None, None, ("row", "col")),
        check_vma=False,
    )
```

```python
import math

import jax
import jax.numpy as jnp
from jax import lax
from jax.experimental import pallas as pl
from jax.experimental.pallas import tpu as pltpu
from jax.sharding import PartitionSpec as P

HEADS = 16
HEAD = 48
D_TOK = 768
HEADS_A = 4
HEAD_A = 32
C_ATOM = 128
Q_WIN = 32
K_WIN = 128
MARGIN = 48
BLOCKS = 2
SAMPLES = 2
TOK_DEV = 16
A_DEV = 128
ROWS = 16
COLS = 8
DEVICES = ROWS * COLS
QUERIES = COLS * TOK_DEV
KEYS = ROWS * TOK_DEV
PART = D_TOK + 128
STRIDE = QUERIES + 8
LN_EPSILON = 1e-05
LOG2E = math.log2(math.e)
MESH = pl.DeviceIdType.MESH
F32 = jnp.float32
BF16 = jnp.bfloat16

HEAD_TILES = ((0, 1), (0, 1), (0, 2), (1, 1), (1, 1), (1, 2), (2, 1), (2, 1))


def dot(a, b, dims=((1,), (0,)), precision=None):
    return lax.dot_general(
        a, b, (dims, ((), ())), precision=precision, preferred_element_type=F32
    )


def iota(shape, dim):
    return lax.broadcasted_iota(jnp.int32, shape, dim)


def layer_norm(v):
    mean = jnp.mean(v, axis=-1, keepdims=True)
    centred = v - mean
    var = jnp.mean(centred * centred, axis=-1, keepdims=True)
    return centred * lax.rsqrt(var + LN_EPSILON)


def swap2(i):
    return i + 2 - 4 * lax.rem(lax.div(i, 2), 2)


def kernel(
    noise_level_hbm,
    atom_pos_hbm,
    noise_hbm,
    atom_single_hbm,
    w_pos_hbm,
    atom_bias_hbm,
    atom_qkv_hbm,
    atom_out_hbm,
    w_agg_hbm,
    atom_token_hbm,
    token_counts_hbm,
    pair_hbm,
    w_pairbias_hbm,
    tok_proj_hbm,
    tok_out_hbm,
    w_dec_hbm,
    w_update_hbm,
    out,
    noise_level,
    atom_pos,
    noise,
    atom_single,
    w_pos,
    atom_bias,
    atom_qkv,
    atom_out,
    w_agg,
    atom_token,
    token_counts,
    w_pairbias,
    w_dec,
    w_update,
    pair,
    proj,
    tok_out,
    bias,
    w_spread,
    centre,
    expand,
    atom_enc,
    queries_a,
    kv_own,
    halo,
    kv_pad,
    spill_out,
    spill_in,
    token_act,
    gates,
    q_all,
    kv_all,
    q_ref,
    k_ref,
    v_ref,
    stat,
    part,
    part_in,
    dec_out,
    dec_in,
    input_sem,
    pair_sem,
    weight_sem,
    halo_send,
    halo_recv,
    spill_sems,
    dec_sems,
    turn_send,
    turn_recv,
    q_send,
    q_recv,
    kv_send,
    kv_recv,
    twin_send,
    twin_recv,
    part_send,
    part_recv,
):
    r = lax.axis_index("row")
    c = lax.axis_index("col")
    d = r * COLS + c
    up = lax.rem(d + 1, DEVICES)
    down = lax.rem(d + DEVICES - 1, DEVICES)
    up_id = (lax.div(up, COLS), lax.rem(up, COLS))
    down_id = (lax.div(down, COLS), lax.rem(down, COLS))
    core = lax.rem(r, 2)
    level_r = lax.div(r, 2)
    twin_id = (r + 1 - 2 * core, c)
    turn_to = (2 * swap2(c) + core, level_r)
    turn_from = (2 * c + core, swap2(level_r))
    slot = core * COLS + swap2(level_r)
    turn_slot = core * COLS + c

    barrier = pltpu.get_barrier_semaphore()

    def greet(device):
        pl.semaphore_signal(barrier, inc=1, device_id=device, device_id_type=MESH)

    def each(first, last, act):
        def step(j, _):
            act(j)
            return 0

        lax.fori_loop(first, last, step, 0)

    greet(turn_from)
    greet(up_id)
    greet(down_id)
    each(1, COLS, lambda j: greet((r, lax.rem(c + j, COLS))))
    each(1, ROWS // 2, lambda j: greet((lax.rem(r + 2 * j, ROWS), c)))
    greet(twin_id)

    small = [
        (noise_level_hbm, noise_level),
        (atom_pos_hbm, atom_pos),
        (noise_hbm, noise),
        (atom_single_hbm, atom_single),
        (w_pos_hbm, w_pos),
        (atom_qkv_hbm, atom_qkv),
        (w_pairbias_hbm, w_pairbias),
        (atom_bias_hbm, atom_bias),
        (atom_out_hbm, atom_out),
        (w_agg_hbm, w_agg),
        (atom_token_hbm, atom_token),
        (token_counts_hbm, token_counts),
        (w_dec_hbm, w_dec),
        (w_update_hbm, w_update),
    ]
    small_copies = [
        pltpu.make_async_copy(a, b, input_sem.at[i]) for i, (a, b) in enumerate(small)
    ]
    for copy in small_copies:
        copy.start()

    def pair_copy(i):
        rows = pl.ds(i * 32, 32)
        return pltpu.make_async_copy(pair_hbm.at[rows], pair.at[rows], pair_sem.at[i])

    proj_copies = [
        pltpu.make_async_copy(tok_proj_hbm.at[b], proj.at[b], weight_sem.at[b]) for b in range(2)
    ]
    out_copies = [
        pltpu.make_async_copy(tok_out_hbm.at[b], tok_out.at[b], weight_sem.at[2 + b])
        for b in range(2)
    ]
    for i in range(4):
        pair_copy(i).start()
    for b in range(2):
        proj_copies[b].start()
        out_copies[b].start()
    for copy in small_copies[:7]:
        copy.wait()

    row_i, col_i = iota((KEYS, KEYS), 0), iota((KEYS, KEYS), 1)
    same = row_i // C_ATOM == col_i // C_ATOM
    centre[...] = (
        jnp.where(row_i == col_i, 1.0, 0.0) - jnp.where(same, 1.0 / C_ATOM, 0.0)
    ).astype(BF16)
    heads_wide = iota((2 * HEADS, KEYS), 1) // 8 == iota((2 * HEADS, KEYS), 0)
    wide = dot(w_pairbias[...], jnp.where(heads_wide, 1.0, 0.0).astype(BF16), ((0,), (0,)))
    query_of = lax.rem(iota((C_ATOM, KEYS), 1), 8)
    for q in range(8):
        w_spread[q * C_ATOM : (q + 1) * C_ATOM, :] = jnp.where(query_of == q, wide, 0.0).astype(
            BF16
        )

    def pair_bias(first, last):
        def step(i, _):
            q0 = pl.multiple_of(i * 8, 8)
            centred, squares = [], []
            for p in range(4):
                two = jnp.concatenate([pair[q0 + 2 * p], pair[q0 + 2 * p + 1]], axis=1)
                part_centred = dot(two, centre[...])
                centred.append(part_centred.astype(BF16))
                squares.append(part_centred * part_centred)
            y = dot(jnp.concatenate(centred, axis=1), w_spread[...])
            query = lax.rem(iota((KEYS, C_ATOM), 1), 8)
            total = jnp.zeros((KEYS, C_ATOM), F32)
            for q in range(8):
                half = slice((q % 2) * C_ATOM, (q % 2 + 1) * C_ATOM)
                mine = jnp.sum(squares[q // 2][:, half], axis=1, keepdims=True)
                total = jnp.where(query == q, mine, total)
            scale = lax.rsqrt(total * (1.0 / C_ATOM) + LN_EPSILON) * LOG2E
            turned = (y * jnp.concatenate([scale, scale], axis=1)).T
            for t in range(KEYS // 128):
                for h in range(2 * HEADS):
                    bias[t, pl.ds(pl.multiple_of(h * STRIDE + q0, 8), 8), :] = turned[
                        h * 8 : (h + 1) * 8, t * 128 : (t + 1) * 128
                    ]
            return 0

        lax.fori_loop(first, last, step, 0)

    acts = []
    for s in range(SAMPLES):
        level = jnp.broadcast_to(noise_level[:, s : s + 1], (1, A_DEV))
        noisy = atom_pos[:, s] + level * noise[:, s]
        scaled = noisy / jnp.sqrt(level * level + 1.0)
        acts.append(
            atom_single[...].astype(F32)
            + dot(scaled, w_pos[...], ((0,), (0,)), lax.Precision.HIGHEST)
        )
    act = jnp.concatenate(acts, axis=0)
    atom_enc[...] = act
    projected = dot(layer_norm(act).astype(BF16), atom_qkv[...]).astype(BF16)
    for s in range(SAMPLES):
        rows = slice(s * A_DEV, (s + 1) * A_DEV)
        queries_a[s] = projected[rows, 0:C_ATOM]
        kv_own[s] = projected[rows, C_ATOM:]
    pl.semaphore_wait(barrier, 1 + 2 + (COLS - 1) + (ROWS // 2 - 1) + 1)

    def halo_copies():
        return (
            pltpu.make_async_remote_copy(
                src_ref=kv_own.at[:, pl.ds(A_DEV - MARGIN, MARGIN)],
                dst_ref=halo.at[0],
                send_sem=halo_send.at[0],
                recv_sem=halo_recv.at[0],
                device_id=up_id,
                device_id_type=MESH,
            ),
            pltpu.make_async_remote_copy(
                src_ref=kv_own.at[:, pl.ds(0, MARGIN)],
                dst_ref=halo.at[1],
                send_sem=halo_send.at[1],
                recv_sem=halo_recv.at[1],
                device_id=down_id,
                device_id_type=MESH,
            ),
        )

    to_up, to_down = halo_copies()
    to_up.start()
    to_down.start()
    for i in range(4):
        pair_copy(i).wait()
    pair_bias(0, 6)
    for copy in small_copies[7:]:
        copy.wait()
    to_up.wait()
    to_down.wait()
    for s in range(SAMPLES):
        kv_pad[s, 0:MARGIN] = halo[0, s]
        kv_pad[s, MARGIN : MARGIN + A_DEV] = kv_own[s]
        kv_pad[s, MARGIN + A_DEV : A_DEV + 2 * MARGIN] = halo[1, s]

    lane_head = iota((HEADS_A, Q_WIN, C_ATOM), 2) // HEAD_A == iota((HEADS_A, Q_WIN, C_ATOM), 0)
    head_mask = jnp.where(lane_head, 1.0, 0.0)
    head_mask_low = head_mask.astype(BF16)
    slots = iota((1, K_WIN), 1)
    windows = [(s, w) for s in range(SAMPLES) for w in range(A_DEV // Q_WIN)]
    scores = []
    for s, w in windows:
        rows = slice(w * Q_WIN, (w + 1) * Q_WIN)
        keys = kv_pad[s, w * Q_WIN : w * Q_WIN + K_WIN, 0:C_ATOM]
        query = (queries_a[s, rows][None] * head_mask_low).reshape(HEADS_A * Q_WIN, C_ATOM)
        scores.append(dot(query, keys, ((1,), (1,))))
    weights = []
    for (s, w), score in zip(windows, scores):
        rows = slice(w * Q_WIN, (w + 1) * Q_WIN)
        score = score * (1 / math.sqrt(HEAD_A))
        score = score + atom_bias[:, rows, :].astype(F32).reshape(HEADS_A * Q_WIN, K_WIN)
        index = d * A_DEV + w * Q_WIN - MARGIN + slots
        inside = (index >= 0) & (index < DEVICES * A_DEV)
        score = jnp.where(inside, score, -1e30)
        p = jnp.exp(score - jnp.max(score, axis=-1, keepdims=True))
        weights.append((p.astype(BF16), jnp.sum(p, axis=-1, keepdims=True)))
    mixed = []
    for (s, w), (p, total) in zip(windows, weights):
        mix = dot(p, kv_pad[s, w * Q_WIN : w * Q_WIN + K_WIN, C_ATOM:]) / total
        mixed.append(jnp.sum(mix.reshape(HEADS_A, Q_WIN, C_ATOM) * head_mask, axis=0))
    atom_enc[...] = atom_enc[...] + dot(
        jnp.concatenate(mixed, axis=0).astype(BF16), atom_out[...]
    )

    slot_index = atom_token[...] - (d * TOK_DEV - TOK_DEV)
    member = jnp.where(
        slot_index == iota((2 * TOK_DEV, A_DEV), 0), 1.0, 0.0
    )
    member_low = member.astype(BF16)
    hidden = jnp.maximum(dot(atom_enc[...].astype(BF16), w_agg[...]), 0.0)
    for s in range(SAMPLES):
        mine = hidden[s * A_DEV : (s + 1) * A_DEV]
        high = mine.astype(BF16)
        low = (mine - high.astype(F32)).astype(BF16)
        sums = dot(
            jnp.concatenate([member_low, member_low], axis=1),
            jnp.concatenate([high, low], axis=0),
        )
        spill_out[s] = sums[0:TOK_DEV].astype(BF16)
        token_act[s] = sums[TOK_DEV : 2 * TOK_DEV]
    spill = pltpu.make_async_remote_copy(
        src_ref=spill_out,
        dst_ref=spill_in,
        send_sem=spill_sems.at[0],
        recv_sem=spill_sems.at[1],
        device_id=down_id,
        device_id_type=MESH,
    )
    spill.start()
    pair_bias(6, 11)
    lanes = iota((D_TOK, 2 * C_ATOM), 0)
    head_of = lax.rem(iota((D_TOK, 2 * C_ATOM), 1), C_ATOM)
    expand[...] = jnp.where(
        (lanes >= head_of * HEAD) & (lanes < head_of * HEAD + HEAD), 1.0, 0.0
    ).astype(BF16)
    diagonal = iota((TOK_DEV, TOK_DEV), 0) == iota((TOK_DEV, TOK_DEV), 1)
    counts = jnp.sum(
        jnp.where(diagonal, token_counts[...].astype(F32), 0.0), axis=1, keepdims=True
    )
    spill.wait()
    for s in range(SAMPLES):
        token_act[s] = (token_act[s] + spill_in[s].astype(F32)) / counts

    def q_copy(b, s, j):
        return pltpu.make_async_remote_copy(
            src_ref=q_all.at[b, s, c],
            dst_ref=q_all.at[b, s, c],
            send_sem=q_send.at[b, s, j],
            recv_sem=q_recv.at[b, s, c],
            device_id=(r, lax.rem(c + j, COLS)),
            device_id_type=MESH,
        )

    def q_arrival(b, s, j):
        peer = lax.rem(c + j, COLS)
        return pltpu.make_async_remote_copy(
            src_ref=q_all.at[b, s, peer],
            dst_ref=q_all.at[b, s, peer],
            send_sem=q_send.at[b, s, j],
            recv_sem=q_recv.at[b, s, peer],
            device_id=(r, peer),
            device_id_type=MESH,
        )

    def turn_copy(b, s):
        return pltpu.make_async_remote_copy(
            src_ref=q_all.at[b, s, c],
            dst_ref=kv_all.at[b, s, turn_slot],
            send_sem=turn_send.at[b, s],
            recv_sem=turn_recv.at[b, s],
            device_id=turn_to,
            device_id_type=MESH,
        )

    def turn_arrival(b, s):
        return pltpu.make_async_remote_copy(
            src_ref=q_all.at[b, s, c],
            dst_ref=kv_all.at[b, s, slot],
            send_sem=turn_send.at[b, s],
            recv_sem=turn_recv.at[b, s],
            device_id=turn_from,
            device_id_type=MESH,
        )

    def kv_copy(b, s, j):
        return pltpu.make_async_remote_copy(
            src_ref=kv_all.at[b, s, slot],
            dst_ref=kv_all.at[b, s, slot],
            send_sem=kv_send.at[b, s, j],
            recv_sem=kv_recv.at[b, s, level_r],
            device_id=(lax.rem(r + 2 * j, ROWS), c),
            device_id_type=MESH,
        )

    def kv_arrival(b, s, j):
        peer = lax.rem(r + 2 * j, ROWS)
        peer_slot = core * COLS + swap2(lax.div(peer, 2))
        return pltpu.make_async_remote_copy(
            src_ref=kv_all.at[b, s, peer_slot],
            dst_ref=kv_all.at[b, s, peer_slot],
            send_sem=kv_send.at[b, s, j],
            recv_sem=kv_recv.at[b, s, lax.div(peer, 2)],
            device_id=(peer, c),
            device_id_type=MESH,
        )

    def twin_copy(b, s, half):
        blocks = pl.ds(half * COLS, COLS)
        return pltpu.make_async_remote_copy(
            src_ref=kv_all.at[b, s, blocks],
            dst_ref=kv_all.at[b, s, blocks],
            send_sem=twin_send.at[b, s],
            recv_sem=twin_recv.at[b, s],
            device_id=twin_id,
            device_id_type=MESH,
        )

    def part_copy(b, s, j):
        peer = lax.rem(c + j, COLS)
        return pltpu.make_async_remote_copy(
            src_ref=part.at[b, s, peer],
            dst_ref=part_in.at[b, s, c],
            send_sem=part_send.at[b, s, j],
            recv_sem=part_recv.at[b, s, c],
            device_id=(r, peer),
            device_id_type=MESH,
        )

    def part_arrival(b, s, j):
        peer = lax.rem(c + j, COLS)
        return pltpu.make_async_remote_copy(
            src_ref=part.at[b, s, peer],
            dst_ref=part_in.at[b, s, peer],
            send_sem=part_send.at[b, s, j],
            recv_sem=part_recv.at[b, s, peer],
            device_id=(r, peer),
            device_id_type=MESH,
        )

    def send_normed(b, s):
        q_all[b, s, c] = layer_norm(token_act[s]).astype(BF16)
        turn_copy(b, s).start()

    def send_queries(b, s):
        each(0, COLS - 1, lambda j: q_copy(b, s, COLS - 1 - j).start())

    def pass_on(b, s):
        turn_arrival(b, s).wait_recv()
        each(0, ROWS // 2 - 1, lambda j: kv_copy(b, s, ROWS // 2 - 1 - j).start())

    def gate(b, s):
        g = dot(q_all[b, s, c], proj[b, :, 3 * D_TOK :]).astype(BF16).astype(F32)
        gates[s] = 1.0 / (1.0 + jnp.exp(-g))

    def project_queries(b, s):
        each(1, COLS, lambda j: q_arrival(b, s, j).wait_recv())
        normed = q_all[b, s].reshape(QUERIES, D_TOK)
        for n in range(0, D_TOK, 256):
            q_ref[s, :, n : n + 256] = (
                dot(normed, proj[b, :, n : n + 256]) * (LOG2E / math.sqrt(HEAD))
            ).astype(BF16)

    def share(b, s):
        each(1, ROWS // 2, lambda j: kv_arrival(b, s, j).wait_recv())
        twin_copy(b, s, core).start()

    def project_keys(b, s, half):
        normed = kv_all[b, s, pl.ds(half * COLS, COLS)].reshape(KEYS // 2, D_TOK)
        rows = pl.ds(pl.multiple_of(half * (KEYS // 2), KEYS // 2), KEYS // 2)
        for n in range(0, D_TOK, 256):
            at = D_TOK + n
            k_ref[s, n : n + 256, rows] = dot(normed, proj[b, :, at : at + 256]).T.astype(BF16)
            at = 2 * D_TOK + n
            v_ref[s, rows, n : n + 256] = dot(normed, proj[b, :, at : at + 256]).astype(BF16)

    def attention(b, s):
        project_keys(b, s, core)
        twin_copy(b, s, 1 - core).wait_recv()
        project_keys(b, s, 1 - core)
        stat[...] = jnp.zeros_like(stat)
        lane = iota((QUERIES, C_ATOM), 1)

        def group(g, _):
            base = g * (8 * HEAD)
            outs = []
            stats = stat[...]
            for hh, (tile, tiles) in enumerate(HEAD_TILES):
                window = pl.ds(base + tile * 128, tiles * 128)
                at = iota((16, tiles * 128), 1) + tile * 128
                mine = jnp.where((at >= hh * HEAD) & (at < (hh + 1) * HEAD), 1.0, 0.0)
                query = q_ref[s, :, window].reshape(QUERIES // 16, 16, tiles * 128)
                query = (query * mine.astype(BF16)[None]).reshape(QUERIES, tiles * 128)
                rows = pl.ds((b * HEADS + g * 8 + hh) * STRIDE, QUERIES)
                score = dot(query, k_ref[s, window, :]) + jnp.concatenate(
                    [bias[t, rows, :] for t in range(KEYS // 128)], axis=1
                )
                top = jnp.max(score, axis=-1, keepdims=True)
                p = jnp.exp2(score - top)
                total = jnp.sum(p, axis=-1, keepdims=True)
                outs.append(dot(p.astype(BF16), v_ref[s, :, window]))
                stats = jnp.where(lane == g * 8 + hh, top, stats)
                stats = jnp.where(lane == HEADS + g * 8 + hh, total, stats)
            stat[...] = stats
            o0, o1, o2, o3, o4, o5, o6, o7 = outs
            tiles = (
                jnp.where(lane < 48, o0, jnp.where(lane < 96, o1, o2[:, :128])),
                jnp.where(
                    lane < 16,
                    o2[:, 128:],
                    jnp.where(lane < 64, o3, jnp.where(lane < 112, o4, o5[:, :128])),
                ),
                jnp.where(lane < 32, o5[:, 128:], jnp.where(lane < 80, o6, o7)),
            )
            for t, value in enumerate(tiles):
                where = pl.ds(base + t * 128, 128)
                part[b, s, :, :, where] = value.astype(BF16).reshape(COLS, TOK_DEV, 128)
            return 0

        group(0, 0)
        group(1, 0)
        exact = stat[...]
        high = exact.astype(BF16).astype(F32)
        rest = exact - high
        mid = rest.astype(BF16).astype(F32)
        pieces = high + pltpu.roll(mid, 32, 1) + pltpu.roll(rest - mid, 64, 1)
        part[b, s, :, :, D_TOK:PART] = pieces.astype(BF16).reshape(COLS, TOK_DEV, 128)
        each(0, COLS - 1, lambda j: part_copy(b, s, COLS - 1 - j).start())
        part_in[b, s, c] = part[b, s, c]

    def combine(b, s):
        each(1, COLS, lambda j: part_arrival(b, s, j).wait_recv())
        pieces = part_in[b, s, :, :, D_TOK:PART].astype(F32).reshape(QUERIES, 128)
        stats = pieces + pltpu.roll(pieces, 96, 1) + pltpu.roll(pieces, 64, 1)
        stats = stats.reshape(COLS, TOK_DEV, 128)
        weight = jnp.exp2(stats - jnp.max(stats, axis=0, keepdims=True))
        dens = pltpu.roll(stats.reshape(QUERIES, 128), 128 - HEADS, 1).reshape(stats.shape)
        total = jnp.sum(weight * dens, axis=0, keepdims=True)
        weight = jnp.where(iota(stats.shape, 2) < HEADS, weight / total, 0.0)
        weight = weight.reshape(QUERIES, 128)
        high = weight.astype(BF16)
        low = (weight - high.astype(F32)).astype(BF16)
        spread = dot(jnp.concatenate([high, low], axis=1), expand[...], ((1,), (1,)))
        nums = part_in[b, s, :, :, 0:D_TOK].astype(F32)
        mix = jnp.sum(nums * spread.reshape(COLS, TOK_DEV, D_TOK), axis=0)
        gated = (gates[s] * mix).astype(BF16)
        token_act[s] = token_act[s] + dot(gated, tok_out[b])

    samples = range(SAMPLES)
    for s in samples:
        send_normed(0, s)
    for s in samples:
        send_queries(0, s)
    pair_bias(11, 16)
    for b in range(BLOCKS):
        for s in samples:
            pass_on(b, s)
        proj_copies[b].wait()
        for s in samples:
            gate(b, s)
        for s in samples:
            project_queries(b, s)
        for s in samples:
            share(b, s)
        for s in samples:
            attention(b, s)
        out_copies[b].wait()
        for s in samples:
            combine(b, s)
            if b + 1 < BLOCKS:
                send_normed(b + 1, s)
                send_queries(b + 1, s)

    for s in range(SAMPLES):
        dec_out[s] = dot(token_act[s].astype(BF16), w_dec[...])
    decoded = pltpu.make_async_remote_copy(
        src_ref=dec_out,
        dst_ref=dec_in,
        send_sem=dec_sems.at[0],
        recv_sem=dec_sems.at[1],
        device_id=up_id,
        device_id_type=MESH,
    )
    decoded.start()
    for b in range(BLOCKS):
        for s in range(SAMPLES):
            each(1, COLS, lambda j: q_copy(b, s, j).wait_send())
            turn_copy(b, s).wait_send()
            each(1, ROWS // 2, lambda j: kv_copy(b, s, j).wait_send())
            twin_copy(b, s, core).wait_send()
            each(1, COLS, lambda j: part_copy(b, s, j).wait_send())

    decoded.wait()
    member3 = jnp.concatenate([member_low] * 3, axis=0)
    for s in range(SAMPLES):
        table = jnp.concatenate([dec_in[s], dec_out[s]], axis=0)
        high = table.astype(BF16)
        rest = table - high.astype(F32)
        mid = rest.astype(BF16)
        low = (rest - mid.astype(F32)).astype(BF16)
        picked = dot(member3, jnp.concatenate([high, mid, low], axis=0), ((0,), (0,)))
        atom_dec = atom_enc[s * A_DEV : (s + 1) * A_DEV] + picked
        update = dot(w_update[...], layer_norm(atom_dec).astype(BF16), ((1,), (1,)))
        level = jnp.broadcast_to(noise_level[:, s : s + 1], (1, A_DEV))
        noisy = atom_pos[:, s] + level * noise[:, s]
        square = level * level + 1.0
        out[:, s] = noisy / square + level / jnp.sqrt(square) * update


def body(
    atom_pos,
    noise,
    noise_level,
    atom_single,
    w_pos,
    atom_bias,
    atom_qkv,
    atom_out,
    w_agg,
    atom_token,
    token_counts,
    pair,
    w_pairbias,
    tok_proj,
    tok_out,
    w_dec,
    w_update,
):
    vmem = pl.BlockSpec(memory_space=pltpu.VMEM)
    hbm = pl.BlockSpec(memory_space=pl.ANY)
    dma = pltpu.SemaphoreType.DMA
    denoised = pl.pallas_call(
        kernel,
        out_shape=jax.ShapeDtypeStruct((3, SAMPLES, A_DEV), F32),
        in_specs=[hbm] * 17,
        out_specs=vmem,
        scratch_shapes=[
            pltpu.VMEM((1, SAMPLES), F32),
            pltpu.VMEM((3, SAMPLES, A_DEV), F32),
            pltpu.VMEM((3, SAMPLES, A_DEV), F32),
            pltpu.VMEM((A_DEV, C_ATOM), BF16),
            pltpu.VMEM((3, C_ATOM), F32),
            pltpu.VMEM((HEADS_A, A_DEV, K_WIN), BF16),
            pltpu.VMEM((C_ATOM, 3 * C_ATOM), BF16),
            pltpu.VMEM((C_ATOM, C_ATOM), BF16),
            pltpu.VMEM((C_ATOM, D_TOK), BF16),
            pltpu.VMEM((1, A_DEV), jnp.int32),
            pltpu.VMEM((1, TOK_DEV), jnp.int32),
            pltpu.VMEM((2 * HEADS, C_ATOM), BF16),
            pltpu.VMEM((D_TOK, C_ATOM), BF16),
            pltpu.VMEM((3, C_ATOM), BF16),
            pltpu.VMEM((QUERIES, KEYS, C_ATOM), BF16),
            pltpu.VMEM((BLOCKS, D_TOK, 4 * D_TOK), BF16),
            pltpu.VMEM((BLOCKS, D_TOK, D_TOK), BF16),
            pltpu.VMEM((KEYS // 128, 2 * HEADS * STRIDE, 128), F32),
            pltpu.VMEM((8 * C_ATOM, KEYS), BF16),
            pltpu.VMEM((KEYS, KEYS), BF16),
            pltpu.VMEM((D_TOK, 2 * C_ATOM), BF16),
            pltpu.VMEM((SAMPLES * A_DEV, C_ATOM), F32),
            pltpu.VMEM((SAMPLES, A_DEV, C_ATOM), BF16),
            pltpu.VMEM((SAMPLES, A_DEV, 2 * C_ATOM), BF16),
            pltpu.VMEM((2, SAMPLES, MARGIN, 2 * C_ATOM), BF16),
            pltpu.VMEM((SAMPLES, A_DEV + 2 * MARGIN, 2 * C_ATOM), BF16),
            pltpu.VMEM((SAMPLES, TOK_DEV, D_TOK), BF16),
            pltpu.VMEM((SAMPLES, TOK_DEV, D_TOK), BF16),
            pltpu.VMEM((SAMPLES, TOK_DEV, D_TOK), F32),
            pltpu.VMEM((SAMPLES, TOK_DEV, D_TOK), F32),
            pltpu.VMEM((BLOCKS, SAMPLES, COLS, TOK_DEV, D_TOK), BF16),
            pltpu.VMEM((BLOCKS, SAMPLES, ROWS, TOK_DEV, D_TOK), BF16),
            pltpu.VMEM((SAMPLES, QUERIES, D_TOK), BF16),
            pltpu.VMEM((SAMPLES, D_TOK, KEYS), BF16),
            pltpu.VMEM((SAMPLES, KEYS, D_TOK), BF16),
            pltpu.VMEM((QUERIES, 128), F32),
            pltpu.VMEM((BLOCKS, SAMPLES, COLS, TOK_DEV, PART), BF16),
            pltpu.VMEM((BLOCKS, SAMPLES, COLS, TOK_DEV, PART), BF16),
            pltpu.VMEM((SAMPLES, TOK_DEV, C_ATOM), F32),
            pltpu.VMEM((SAMPLES, TOK_DEV, C_ATOM), F32),
            dma((14,)),
            dma((4,)),
            dma((4,)),
            dma((2,)),
            dma((2,)),
            dma((2,)),
            dma((2,)),
            dma((BLOCKS, SAMPLES)),
            dma((BLOCKS, SAMPLES)),
            dma((BLOCKS, SAMPLES, COLS)),
            dma((BLOCKS, SAMPLES, COLS)),
            dma((BLOCKS, SAMPLES, ROWS // 2)),
            dma((BLOCKS, SAMPLES, ROWS // 2)),
            dma((BLOCKS, SAMPLES)),
            dma((BLOCKS, SAMPLES)),
            dma((BLOCKS, SAMPLES, COLS)),
            dma((BLOCKS, SAMPLES, COLS)),
        ],
        compiler_params=pltpu.CompilerParams(
            collective_id=0, has_side_effects=True, vmem_limit_bytes=56 * 1024 * 1024
        ),
    )(
        noise_level.reshape(1, SAMPLES),
        atom_pos.transpose(1, 0, 2),
        noise.transpose(1, 0, 2),
        atom_single,
        w_pos,
        atom_bias,
        atom_qkv,
        atom_out,
        w_agg,
        atom_token.reshape(1, A_DEV),
        token_counts.reshape(1, TOK_DEV),
        pair,
        w_pairbias.T,
        tok_proj,
        tok_out,
        w_dec,
        w_update.T,
    )
    return denoised.transpose(1, 0, 2)


def solution(mesh):
    return jax.shard_map(
        body,
        mesh=mesh,
        in_specs=(
            P(None, None, ("row", "col")),
            P(None, None, ("row", "col")),
            P(),
            P(("row", "col"), None),
            P(),
            P(None, ("row", "col"), None),
            P(),
            P(),
            P(),
            P(("row", "col")),
            P(("row", "col")),
            P("row", "col", None),
            P(),
            P(),
            P(),
            P(),
            P(),
        ),
        out_specs=P(None, None, ("row", "col")),
        check_vma=False,
    )
```
